512 devices in a mesh: scene: 32 (over x, z_hi, core), view: 16 (over z_lo, y).
Axes of the slice: x: 4, y: 4, z: 16 (z_hi: 4, z_lo: 4; z = z_hi * 4 + z_lo), core: 2. Of those that a mesh axis runs over, the one named last changes fastest.
Arguments:
- query_rows: bfloat16 [32, 16, 256, 512], P('scene', 'view'), may hold values from -270 to 270, as said below
- key_rows: bfloat16 [32, 16, 256, 512], P('scene', 'view'), may hold values from -7 to 7, as said below
- value_rows: bfloat16 [32, 16, 256, 512], P('scene', 'view'), may hold values from -24 to 24
- grad_out: bfloat16 [32, 16, 256, 1024], P('scene', 'view'), may hold values from -24 to 24
- out_weight: bfloat16 [512, 1024], replicated, may hold values from -0.25 to 0.25
- fetch_list: int32 [32, 16, 16], P('scene'), may hold values from 0 to 1
- read_mask: int32 [32, 16, 2, 16], P('scene', 'view'), may hold values 0 or 1
Outputs:
- layer_out: bfloat16 [32, 16, 256, 1024], P('scene', 'view')
- grad_query: bfloat16 [32, 16, 256, 512], P('scene', 'view')
- grad_key: bfloat16 [32, 16, 256, 512], P('scene', 'view')
- grad_value: bfloat16 [32, 16, 256, 512], P('scene', 'view')
- grad_weight: float32 [512, 1024], P('scene', 'view')
The draws below stay inside these ranges and needn't reach their ends.
Inputs may be any that keep to these rules, and one draw needn't show every extreme that they name: `query_rows`: queries of order one; some rows may be large multiples of other rows of keys. `key_rows`: keys of order one.
All inputs are finite; a program needn't handle non-finite values. No bound on the sum of `read_mask` on one device may be relied on, other than what follows from the above.
Results may differ from the reference program's by a relative error of at most 0.029.
Values may be sent and summed in bfloat16 or wider, within the bound.
No kernel may reach another device: no remote copies, remote signals or barrier semaphores. Data moves between devices by JAX's collectives and lax.ppermute only.
A program may use at most 128 MiB of HBM per device.

```python
import jax
import jax.numpy as jnp
from jax import lax

D = 1024
HEADS = 8
HEAD_DIM = 64
BLK = 128
TOK = 256
INNER = 512
NBLK = 2
VIEWS = 16
SCENES = 32


def shared_base(key):
    return jnp.clip(jax.random.normal(key, (SCENES, VIEWS, TOK, INNER), jnp.float32), -6.0, 6.0)


def draw_key_rows(key, part):
    base = shared_base(key)
    return base.astype(jnp.bfloat16)


def draw_query_rows(key, part):
    key = jax.random.fold_in(key, 5)
    own_rows = jnp.clip(jax.random.normal(key, (SCENES, VIEWS, TOK, INNER), jnp.float32), -6.0, 6.0)
    return own_rows.astype(jnp.bfloat16)


def place_ends(entries, own_key, smallest, top_value):
    longest = entries.shape.index(max(entries.shape))
    spots = []
    for shift in (0, 1):
        where = [jax.random.randint(jax.random.fold_in(own_key, axis), (), 0, length) for axis, length in enumerate(entries.shape)]
        where[longest] = (where[longest] + shift) % entries.shape[longest]
        spots.append(tuple(where))
    return entries.at[spots[0]].set(smallest).at[spots[1]].set(top_value)


def raised(values, rng, source, target, parts, factor):
    owner, partner = [(jnp.arange(values.shape[position]) // (values.shape[position] // parts)).reshape([-1 if axis == position else 1 for axis in range(values.ndim)]) for position in (source, target)]
    chosen = jax.random.permutation(rng, parts)[partner]
    strong = (owner == chosen) | (owner == (partner + parts // 2) % parts)
    return jnp.where(strong, factor * values, values)


def shard_levels(stream_key, dims, shards, low, top_value):
    def one(dim, parts):
        steps = jax.random.uniform(jax.random.fold_in(jax.random.fold_in(stream_key, 6), dim), (parts,), jnp.float32, low / len(shards), top_value / len(shards))
        return jnp.repeat(jnp.exp(steps), dims[dim] // parts).reshape((-1,) + (1,) * (len(dims) - dim - 1))

    level = one(*shards[0])
    for cut in shards[1:]:
        level = level * one(*cut)
    return level


def centred(key, dims, deviation, most, cuts=(), kind=jnp.bfloat16):
    entries = deviation * jax.random.normal(key, dims, jnp.float32)
    if cuts:
        entries = entries * shard_levels(key, dims, cuts, -0.22, 0.18)
    return jnp.clip(entries, -most, most).astype(kind)


def bell_draw_with(rng, extent, spread, bound, cuts, heavy, kind=jnp.bfloat16):
    entries = spread * jax.random.normal(rng, extent, jnp.float32)
    if cuts:
        entries = entries * shard_levels(rng, extent, cuts, -0.22, 0.18)
    return jnp.clip(raised(entries, jax.random.fold_in(rng, 3), *heavy), -bound, bound).astype(kind)


def setup_inputs(seed: int = 0) -> dict:
    streams_of = jax.random.split(jax.random.key(seed), 8)
    return {
        "query_rows": draw_query_rows(jax.random.fold_in(streams_of[7], 71), 0),
        "key_rows": draw_key_rows(jax.random.fold_in(streams_of[7], 71), 0),
        "value_rows": centred(streams_of[2], (SCENES, VIEWS, TOK, INNER), 4.0, 24.0, ((0, 32), (1, 16))),
        "grad_out": bell_draw_with(streams_of[3], (SCENES, VIEWS, TOK, D), 4.0, 24.0, ((0, 32), (1, 16)), (1, 3, 16, 2.0)),
        "out_weight": centred(streams_of[4], (INNER, D), INNER ** -0.5, 0.25),
        "fetch_list": place_ends(jax.random.randint(streams_of[5], (SCENES, VIEWS, VIEWS), 0, TOK // BLK), jax.random.fold_in(streams_of[5], 1), 0, (TOK // BLK) - 1).astype(jnp.int32),
        "read_mask": place_ends((jax.random.randint(streams_of[6], (SCENES, VIEWS, NBLK, VIEWS), 0, 3) < 2).astype(jnp.int32), jax.random.fold_in(streams_of[6], 1), 0, 1),
    }


def head_pass(query_head, key_head, value_head, grad_head, visible, score_scale):
    scores = jnp.dot(query_head, key_head.T, preferred_element_type=jnp.float32) * score_scale
    scores = jnp.where(visible, scores, -jnp.inf)
    row_max = jnp.max(scores, axis=1, keepdims=True)
    weights_raw = jnp.exp(scores - row_max)
    attn_prob = weights_raw / jnp.sum(weights_raw, axis=1, keepdims=True)
    prob_low = attn_prob.astype(jnp.bfloat16)
    head_out = jnp.dot(prob_low, value_head, preferred_element_type=jnp.float32)
    grad_prob = jnp.dot(grad_head, value_head.T, preferred_element_type=jnp.float32)
    row_delta = jnp.sum(attn_prob * grad_prob, axis=1, keepdims=True)
    grad_score = (attn_prob * (grad_prob - row_delta) * score_scale).astype(jnp.bfloat16)
    grad_qhead = jnp.dot(grad_score, key_head, preferred_element_type=jnp.float32)
    grad_khead = jnp.dot(grad_score.T, query_head, preferred_element_type=jnp.float32)
    grad_vhead = jnp.dot(prob_low.T, grad_head, preferred_element_type=jnp.float32)
    return head_out, grad_qhead, grad_khead, grad_vhead


def split_heads(rows):
    return rows.reshape(rows.shape[0], HEADS, HEAD_DIM).transpose(1, 0, 2)


def join_heads(rows):
    return rows.transpose(1, 0, 2).reshape(rows.shape[1], HEADS * HEAD_DIM)


def view_pass(query_own, keys_all, values_all, grad_attn, visible):
    score_scale = HEAD_DIM ** -0.5

    def one_head(head_items):
        return head_pass(head_items[0], head_items[1], head_items[2], head_items[3], visible, score_scale)

    results = lax.map(one_head, (split_heads(query_own), split_heads(keys_all), split_heads(values_all), split_heads(grad_attn)))
    return tuple(join_heads(item) for item in results)


def one_scene(scene_items, out_weight):
    queries, keys_scene, values_scene, grads_scene, fetch_scene, reads_scene = scene_items
    grad_attn = jnp.dot(grads_scene.reshape(VIEWS * TOK, D), out_weight.T, preferred_element_type=jnp.float32)
    grad_attn = grad_attn.astype(jnp.bfloat16).reshape(VIEWS, TOK, INNER)
    blocks = jnp.concatenate([keys_scene, values_scene], axis=-1).reshape(VIEWS, NBLK, BLK, 2 * INNER)
    view_ids = jnp.arange(VIEWS, dtype=jnp.int32)

    def one_view(view_index):
        picks = fetch_scene[view_index]
        remote = blocks[view_ids, picks]
        remote_keys = remote[:, :, :INNER].reshape(VIEWS * BLK, INNER)
        remote_values = remote[:, :, INNER:].reshape(VIEWS * BLK, INNER)
        keys_all = jnp.concatenate([keys_scene[view_index], remote_keys], axis=0)
        values_all = jnp.concatenate([values_scene[view_index], remote_values], axis=0)
        others = (reads_scene[view_index] == 1) & (view_ids != view_index)[None, :]
        remote_seen = jnp.repeat(jnp.repeat(others, BLK, axis=0), BLK, axis=1)
        visible = jnp.concatenate([jnp.ones((TOK, TOK), dtype=bool), remote_seen], axis=1)
        attn_full, grad_q, grad_kall, grad_vall = view_pass(queries[view_index], keys_all, values_all, grad_attn[view_index], visible)
        attn_low = attn_full.astype(jnp.bfloat16)
        layer_rows = jnp.dot(attn_low, out_weight, preferred_element_type=jnp.float32).astype(jnp.bfloat16)
        weight_term = jnp.dot(attn_low.T, grads_scene[view_index], preferred_element_type=jnp.float32)
        own_grads = jnp.concatenate([grad_kall[:TOK], grad_vall[:TOK]], axis=1)
        remote_grads = jnp.concatenate([grad_kall[TOK:], grad_vall[TOK:]], axis=1).astype(jnp.bfloat16)
        return layer_rows, grad_q.astype(jnp.bfloat16), own_grads, remote_grads.reshape(VIEWS, BLK, 2 * INNER), weight_term

    layer_rows, grad_q, own_grads, remote_grads, weight_terms = lax.map(one_view, view_ids)
    block_ids = jnp.arange(NBLK, dtype=jnp.int32)
    landing = (fetch_scene[:, :, None] == block_ids[None, None, :]) & (view_ids[:, None] != view_ids[None, :])[:, :, None]
    added = jnp.einsum("vwn,vwbc->wnbc", landing.astype(jnp.float32), remote_grads.astype(jnp.float32), precision=lax.Precision.HIGHEST)
    summed = (own_grads + added.reshape(VIEWS, TOK, 2 * INNER)).astype(jnp.bfloat16)
    return layer_rows, grad_q, summed[:, :, :INNER], summed[:, :, INNER:], jnp.sum(weight_terms, axis=0)


def reference(query_rows, key_rows, value_rows, grad_out, out_weight, fetch_list, read_mask):
    def scene_step(scene_items):
        return one_scene(scene_items, out_weight)

    layer_out, grad_query, grad_key, grad_value, weight_terms = lax.map(scene_step, (query_rows, key_rows, value_rows, grad_out, fetch_list, read_mask))
    grad_scale = float(SCENES * VIEWS * TOK) ** -0.5
    grad_weight = jnp.sum(weight_terms, axis=0) * grad_scale
    return layer_out, grad_query, grad_key, grad_value, grad_weight
```

```python
import jax
import jax.numpy as jnp
from jax import lax
from jax.experimental import pallas as pl
from jax.experimental.pallas import tpu as pltpu
from jax.sharding import PartitionSpec as P

HEADS = 8
HEAD_DIM = 64
BLK = 128
TOK = 256
VIEWS = 16
INNER = 512
D = 1024
KEYS = TOK + VIEWS * BLK
BF = jnp.bfloat16
F32 = jnp.float32
SCALE = HEAD_DIM ** (-0.5)
PACK_ROWS = TOK + BLK + 16
BACK_ROWS = TOK + BLK
VMEM = pl.BlockSpec(memory_space=pltpu.VMEM)
SMEM = pl.BlockSpec(memory_space=pltpu.SMEM)


def pack_kernel(q_ref, k_ref, v_ref, go_ref, w_ref, mask_ref, out_ref):
    ga = lax.dot_general(
        go_ref[...], w_ref[...], (((1,), (1,)), ((), ())), preferred_element_type=F32
    ).astype(BF)
    q = q_ref[...] * jnp.asarray(SCALE, BF)
    for h in range(HEADS):
        c = slice(h * HEAD_DIM, (h + 1) * HEAD_DIM)
        kv = jnp.concatenate([k_ref[:, c], v_ref[:, c]], axis=1)
        qg = jnp.concatenate([q[:, c], ga[:, c]], axis=1)
        for p in range(2):
            j = 2 * h + p
            out_ref[j, 0:TOK, :] = kv
            out_ref[j, TOK : TOK + BLK, :] = qg[p * BLK : (p + 1) * BLK, :]
            out_ref[j, TOK + BLK : PACK_ROWS, 0:VIEWS] = jnp.broadcast_to(
                mask_ref[p : p + 1, :], (16, VIEWS)
            ).astype(BF)


def attn_kernel(fetch_ref, mask_ref, in_ref, out_ref, kvt, ksel, ktsel, s_ref, d_ref, x_ref, acc):
    lane = lax.broadcasted_iota(jnp.int32, (BLK, 2 * HEAD_DIM), 1)
    for w in range(VIEWS):
        kvt[:, w * TOK : (w + 1) * TOK] = in_ref[w, 0:TOK, :].T
        acc[w] = jnp.zeros((TOK, 2 * HEAD_DIM), F32)

    def one_view(v, carry):
        qg = in_ref[v, TOK : TOK + BLK, :]
        zero = jnp.zeros_like(qg)
        qg2 = jnp.concatenate(
            [jnp.where(lane < HEAD_DIM, qg, zero), jnp.where(lane >= HEAD_DIM, qg, zero)], axis=0
        )
        ksel[0:TOK, :] = in_ref[v, 0:TOK, :]
        ktsel[:, 0:TOK] = kvt[:, pl.ds(pl.multiple_of(v * TOK, TOK), TOK)]
        for w in range(VIEWS):
            at = pl.multiple_of(fetch_ref[v, w] * BLK, BLK)
            to = slice(TOK + w * BLK, TOK + (w + 1) * BLK)
            ksel[to, :] = in_ref[w, pl.ds(at, BLK), :]
            ktsel[:, to] = kvt[:, pl.ds(pl.multiple_of(w * TOK + at, BLK), BLK)]
        top = None
        for c in range(KEYS // TOK):
            rows = slice(c * TOK, (c + 1) * TOK)
            r = lax.dot_general(
                ksel[rows, :], qg2, (((1,), (1,)), ((), ())), preferred_element_type=F32
            )
            d_ref[rows, :] = r[:, BLK:]
            for half in range(2):
                s = r[half * BLK : (half + 1) * BLK, 0:BLK]
                if c > 0:
                    w = 2 * (c - 1) + half
                    seen = jnp.logical_and(mask_ref[v, w] == 1, w != v)
                    s = s + jnp.where(seen, 0.0, -jnp.inf)
                s_ref[c * TOK + half * BLK : c * TOK + (half + 1) * BLK, :] = s
                best = jnp.max(s.reshape(BLK // 8, 8, BLK), axis=0)
                top = best if top is None else jnp.maximum(top, best)
        top = jnp.max(top, axis=0, keepdims=True)
        total = jnp.zeros((8, BLK), F32)
        delta = jnp.zeros((8, BLK), F32)
        for c in range(KEYS // BLK):
            rows = slice(c * BLK, (c + 1) * BLK)
            e = jnp.exp(s_ref[rows, :] - top)
            s_ref[rows, :] = e
            total = total + jnp.sum(e.reshape(BLK // 8, 8, BLK), axis=0)
            delta = delta + jnp.sum((e * d_ref[rows, :]).reshape(BLK // 8, 8, BLK), axis=0)
        total = jnp.sum(total, axis=0, keepdims=True)
        share = 1.0 / total
        delta = jnp.sum(delta, axis=0, keepdims=True) * share
        for c in range(KEYS // TOK):
            rows = slice(c * TOK, (c + 1) * TOK)
            prob = s_ref[rows, :] * share
            x_ref[rows, 0:BLK] = (prob * (d_ref[rows, :] - delta)).astype(BF)
            x_ref[rows, BLK:] = prob.astype(BF)
            g = jnp.dot(x_ref[rows, :], qg2, preferred_element_type=F32)
            if c == 0:
                acc[v] += g
            else:
                for half in range(2):
                    w = 2 * (c - 1) + half
                    at = pl.multiple_of(fetch_ref[v, w] * BLK, BLK)
                    acc[w, pl.ds(at, BLK), :] += g[half * BLK : (half + 1) * BLK, :]
        o = jnp.dot(ktsel[...], x_ref[...], preferred_element_type=F32)
        both = jnp.concatenate([o[:HEAD_DIM, :BLK] * SCALE, o[HEAD_DIM:, BLK:]], axis=0)
        out_ref[v, TOK:BACK_ROWS, :] = both.T.astype(BF)
        return carry

    lax.fori_loop(0, VIEWS, one_view, 0)
    for w in range(VIEWS):
        out_ref[w, 0:TOK, :] = acc[w].astype(BF)


def finish_kernel(in_ref, go_ref, w_ref, layer_ref, gq_ref, gk_ref, gv_ref, wt_ref, attn):
    for h in range(HEADS):
        c = slice(h * HEAD_DIM, (h + 1) * HEAD_DIM)
        kv = in_ref[2 * h, 0:TOK, :].astype(F32) + in_ref[2 * h + 1, 0:TOK, :].astype(F32)
        kv = kv.astype(BF)
        gk_ref[:, c] = kv[:, :HEAD_DIM]
        gv_ref[:, c] = kv[:, HEAD_DIM:]
        for p in range(2):
            rows = slice(p * BLK, (p + 1) * BLK)
            both = in_ref[2 * h + p, TOK:BACK_ROWS, :]
            gq_ref[rows, c] = both[:, :HEAD_DIM]
            attn[rows, c] = both[:, HEAD_DIM:]
    layer_ref[...] = jnp.dot(attn[...], w_ref[...], preferred_element_type=F32).astype(BF)
    term = lax.dot_general(
        attn[...], go_ref[...], (((0,), (0,)), ((), ())), preferred_element_type=F32
    ).astype(BF)
    wide = D // VIEWS
    for j in range(VIEWS):
        c = slice(j * wide, (j + 1) * wide)
        wt_ref[j, :, 0:wide] = term[: INNER // 2, c]
        wt_ref[j, :, wide:] = term[INNER // 2 :, c]


def params(mib):
    return pltpu.CompilerParams(vmem_limit_bytes=mib * 1024 * 1024)


def on_device(query_rows, key_rows, value_rows, grad_out, out_weight, fetch_list, read_mask):
    go = grad_out[0, 0]
    sent = pl.pallas_call(
        pack_kernel,
        out_shape=jax.ShapeDtypeStruct((VIEWS, PACK_ROWS, 2 * HEAD_DIM), BF),
        in_specs=[VMEM] * 6,
        out_specs=VMEM,
        compiler_params=params(24),
    )(query_rows[0, 0], key_rows[0, 0], value_rows[0, 0], go, out_weight, read_mask[0, 0])
    here = lax.all_to_all(sent, "view", split_axis=0, concat_axis=0, tiled=True)
    reads = here[:, TOK + BLK, :VIEWS].astype(jnp.int32)
    back = pl.pallas_call(
        attn_kernel,
        out_shape=jax.ShapeDtypeStruct((VIEWS, BACK_ROWS, 2 * HEAD_DIM), BF),
        in_specs=[SMEM, SMEM, VMEM],
        out_specs=VMEM,
        scratch_shapes=[
            pltpu.VMEM((2 * HEAD_DIM, VIEWS * TOK), BF),
            pltpu.VMEM((KEYS, 2 * HEAD_DIM), BF),
            pltpu.VMEM((2 * HEAD_DIM, KEYS), BF),
            pltpu.VMEM((KEYS, BLK), F32),
            pltpu.VMEM((KEYS, BLK), F32),
            pltpu.VMEM((KEYS, 2 * BLK), BF),
            pltpu.VMEM((VIEWS, TOK, 2 * HEAD_DIM), F32),
        ],
        compiler_params=params(32),
    )(fetch_list[0], reads, here)
    home = lax.all_to_all(back, "view", split_axis=0, concat_axis=0, tiled=True)
    layer, gq, gk, gv, terms = pl.pallas_call(
        finish_kernel,
        out_shape=(
            jax.ShapeDtypeStruct((TOK, D), BF),
            jax.ShapeDtypeStruct((TOK, INNER), BF),
            jax.ShapeDtypeStruct((TOK, INNER), BF),
            jax.ShapeDtypeStruct((TOK, INNER), BF),
            jax.ShapeDtypeStruct((VIEWS, INNER // 2, 2 * D // VIEWS), BF),
        ),
        in_specs=[VMEM] * 3,
        out_specs=(VMEM,) * 5,
        scratch_shapes=[pltpu.VMEM((TOK, INNER), BF)],
        compiler_params=params(32),
    )(home, go, out_weight)
    scenes = lax.axis_size("scene")
    wide = D // VIEWS
    terms = lax.all_to_all(terms, "view", split_axis=0, concat_axis=0, tiled=True)
    part = jnp.sum(terms.astype(F32), axis=0).astype(BF)
    part = jnp.concatenate([part[:, :wide], part[:, wide:]], axis=0)
    part = part.reshape(scenes, INNER // scenes, wide)
    part = lax.all_to_all(part, "scene", split_axis=0, concat_axis=0, tiled=True)
    share = jnp.sum(part.astype(F32), axis=0) * float(scenes * VIEWS * TOK) ** (-0.5)
    return (layer[None, None], gq[None, None], gk[None, None], gv[None, None], share)


def solution(mesh):
    rows = P("scene", "view", None, None)
    return jax.shard_map(
        on_device,
        mesh=mesh,
        in_specs=(rows, rows, rows, rows, P(), P("scene", None, None), rows),
        out_specs=(rows, rows, rows, rows, P("scene", "view")),
        check_vma=False,
    )
```

```python
import jax
import jax.numpy as jnp
from jax import lax
from jax.experimental import pallas as pl
from jax.experimental.pallas import tpu as pltpu
from jax.sharding import PartitionSpec as P

HEADS = 8
HEAD_DIM = 64
BLK = 128
TOK = 256
VIEWS = 16
INNER = 512
D = 1024
KEYS = TOK + VIEWS * BLK
WIDE = 2 * HEAD_DIM
COLS = D // VIEWS
BF = jnp.bfloat16
F32 = jnp.float32
SCALE = HEAD_DIM ** (-0.5)
ROWS = TOK + BLK
PACK_ROWS = ROWS + 16
BACK_ROWS = TOK + BLK // 2
X, ZHI, CORES = 4, 4, 2
NT = (((1,), (1,)), ((), ()))
VMEM = pl.BlockSpec(memory_space=pltpu.VMEM)
SMEM = pl.BlockSpec(memory_space=pltpu.SMEM)


def pack_kernel(q_ref, k_ref, v_ref, go_ref, w_ref, mask_ref, out_ref):
    ga = lax.dot_general(go_ref[...], w_ref[...], NT, preferred_element_type=F32).astype(BF)
    q = q_ref[...] * jnp.asarray(SCALE, BF)
    for h in range(HEADS):
        c = slice(h * HEAD_DIM, (h + 1) * HEAD_DIM)
        kv = jnp.concatenate([k_ref[:, c], v_ref[:, c]], axis=1)
        qg = jnp.concatenate([q[:, c], ga[:, c]], axis=1)
        for p in range(2):
            j = 2 * h + p
            out_ref[j, 0:TOK, :] = kv
            out_ref[j, TOK:ROWS, :] = qg[p * BLK : (p + 1) * BLK, :]
            out_ref[j, ROWS:PACK_ROWS, 0:VIEWS] = jnp.broadcast_to(
                mask_ref[p : p + 1, :], (16, VIEWS)
            ).astype(BF)


def rows_of(v, w, fetch_ref):
    return pl.ds(pl.multiple_of(fetch_ref[v * VIEWS + w] * BLK, BLK), BLK)


def bias_of(v, w, mask_ref):
    seen = jnp.logical_and(mask_ref[v * VIEWS + w] == 1, w != v)
    return jnp.where(seen, 0.0, -jnp.inf)


def gather_cols(v, src, dst, fetch_ref):
    dst[:, 0:TOK] = src[:, pl.ds(pl.multiple_of(v * TOK, TOK), TOK)]
    for w in range(VIEWS):
        at = pl.multiple_of(w * TOK + fetch_ref[v * VIEWS + w] * BLK, BLK)
        dst[:, TOK + w * BLK : TOK + (w + 1) * BLK] = src[:, pl.ds(at, BLK)]


def side_by_side(t):
    half = BLK // 2
    return jnp.concatenate([t[:, :half], t[:, half:]], axis=0).T


def forward_kernel(
    fetch_ref, mask_ref, in_ref, attn_ref, stat_ref, vt, vsel, s_ref, e_ref
):
    lane = lax.broadcasted_iota(jnp.int32, (BLK, WIDE), 1)
    row = lax.broadcasted_iota(jnp.int32, (WIDE, TOK), 0)
    for w in range(VIEWS):
        t = in_ref[w, 0:TOK, :].T
        vt[:, w * TOK : (w + 1) * TOK] = jnp.where(row < HEAD_DIM, jnp.ones_like(t), t)

    def one_view(v, carry):
        qg = in_ref[v, TOK:ROWS, :]
        qs = jnp.where(lane < HEAD_DIM, qg, jnp.zeros_like(qg))
        gather_cols(v, vt, vsel, fetch_ref)
        top = None
        for c in range(KEYS // BLK):
            rows = slice(c * BLK, (c + 1) * BLK)
            if c < 2:
                keys = in_ref[v, rows, :]
            else:
                keys = in_ref[c - 2, rows_of(v, c - 2, fetch_ref), :]
            s = lax.dot_general(keys, qs, NT, preferred_element_type=F32)
            if c >= 2:
                s = s + bias_of(v, c - 2, mask_ref)
            s_ref[rows, :] = s
            best = jnp.max(s.reshape(BLK // 8, 8, BLK), axis=0)
            top = best if top is None else jnp.maximum(top, best)
        top = jnp.max(top, axis=0, keepdims=True)
        for c in range(KEYS // BLK):
            rows = slice(c * BLK, (c + 1) * BLK)
            e_ref[rows, :] = jnp.exp(s_ref[rows, :] - top).astype(BF)
        o = jnp.dot(vsel[...], e_ref[...], preferred_element_type=F32)
        share = 1.0 / o[0:1, :]
        attn = o[HEAD_DIM:, :] * share
        attn_ref[v, :, :] = side_by_side(attn).astype(BF)
        delta = jnp.sum(attn * qg.T[HEAD_DIM:, :].astype(F32), axis=0, keepdims=True)
        stat_ref[v, 0:1, :] = top
        stat_ref[v, 1:2, :] = share
        stat_ref[v, 2:3, :] = delta
        return carry

    lax.fori_loop(0, VIEWS, one_view, 0)


def backward_kernel(
    fetch_ref, mask_ref, in_ref, stat_ref, out_ref, kt, ksel, x_ref, acc
):
    lane = lax.broadcasted_iota(jnp.int32, (BLK, WIDE), 1)
    for w in range(VIEWS):
        kt[:, w * TOK : (w + 1) * TOK] = in_ref[w, 0:TOK, :].T[:HEAD_DIM, :]
        acc[w] = jnp.zeros((TOK, WIDE), F32)

    def one_view(v, carry):
        qg = in_ref[v, TOK:ROWS, :]
        zero = jnp.zeros_like(qg)
        qg2 = jnp.concatenate(
            [jnp.where(lane < HEAD_DIM, qg, zero), jnp.where(lane >= HEAD_DIM, qg, zero)], axis=0
        )
        gather_cols(v, kt, ksel, fetch_ref)
        top = stat_ref[v, 0:1, :]
        share = stat_ref[v, 1:2, :]
        delta = stat_ref[v, 2:3, :]
        for c in range(KEYS // BLK):
            rows = slice(c * BLK, (c + 1) * BLK)
            if c < 2:
                at = (v, rows)
            else:
                at = (c - 2, rows_of(v, c - 2, fetch_ref))
            r = lax.dot_general(in_ref[at[0], at[1], :], qg2, NT, preferred_element_type=F32)
            s = r[:, 0:BLK]
            if c >= 2:
                s = s + bias_of(v, c - 2, mask_ref)
            prob = jnp.exp(s - top) * share
            x = jnp.concatenate([prob * (r[:, BLK:] - delta), prob], axis=1).astype(BF)
            x_ref[rows, :] = x[:, 0:BLK]
            acc[at[0], at[1], :] += jnp.dot(x, qg2, preferred_element_type=F32)
        o = jnp.dot(ksel[...], x_ref[...], preferred_element_type=F32) * SCALE
        out_ref[v, TOK:BACK_ROWS, :] = side_by_side(o).astype(BF)
        return carry

    lax.fori_loop(0, VIEWS, one_view, 0)
    for w in range(VIEWS):
        out_ref[w, 0:TOK, :] = acc[w].astype(BF)


def project_kernel(core_ref, in_ref, go_ref, w_ref, layer_ref, mine_ref, other_ref, attn, term):
    half = BLK // 2
    for h in range(HEADS):
        c = slice(h * HEAD_DIM, (h + 1) * HEAD_DIM)
        for p in range(2):
            both = in_ref[2 * h + p]
            attn[p * BLK : p * BLK + half, c] = both[:, :HEAD_DIM]
            attn[p * BLK + half : (p + 1) * BLK, c] = both[:, HEAD_DIM:]
    layer_ref[...] = jnp.dot(attn[...], w_ref[...], preferred_element_type=F32).astype(BF)
    term[...] = lax.dot_general(
        attn[...], go_ref[...], (((0,), (0,)), ((), ())), preferred_element_type=F32
    ).astype(BF)
    core = core_ref[0]
    own = INNER // (X * ZHI * CORES)
    for x in range(X):
        for side, ref in ((core, mine_ref), (1 - core, other_ref)):
            for z in range(ZHI):
                at = pl.multiple_of((x * ZHI + z) * CORES * own + side * own, own)
                ref[x, z, :, :] = term[pl.ds(at, own), :]


def unpack_kernel(in_ref, gq_ref, gk_ref, gv_ref):
    half = BLK // 2
    for h in range(HEADS):
        c = slice(h * HEAD_DIM, (h + 1) * HEAD_DIM)
        kv = in_ref[2 * h, 0:TOK, :].astype(F32) + in_ref[2 * h + 1, 0:TOK, :].astype(F32)
        kv = kv.astype(BF)
        gk_ref[:, c] = kv[:, :HEAD_DIM]
        gv_ref[:, c] = kv[:, HEAD_DIM:]
        for p in range(2):
            both = in_ref[2 * h + p, TOK:BACK_ROWS, :]
            gq_ref[p * BLK : p * BLK + half, c] = both[:, :HEAD_DIM]
            gq_ref[p * BLK + half : (p + 1) * BLK, c] = both[:, HEAD_DIM:]


def shape(*dims, dtype=BF):
    return jax.ShapeDtypeStruct(dims, dtype)


def call(kernel, outs, args, smem=0, scratch=(), mib=32, flops=0):
    return pl.pallas_call(
        kernel,
        out_shape=outs,
        in_specs=[SMEM] * smem + [VMEM] * (len(args) - smem),
        out_specs=jax.tree.map(lambda _: VMEM, outs),
        scratch_shapes=[pltpu.VMEM(dims, dtype) for dims, dtype in scratch],
        compiler_params=pltpu.CompilerParams(vmem_limit_bytes=mib * 1024 * 1024),
        cost_estimate=pl.CostEstimate(flops=flops, bytes_accessed=4 << 20, transcendentals=0),
    )(*args)


def forward(fetch, reads, here):
    return call(
        forward_kernel,
        (shape(VIEWS, BLK // 2, WIDE), shape(VIEWS, 8, BLK, dtype=F32)),
        (fetch, reads, here),
        smem=2,
        scratch=[
            ((WIDE, VIEWS * TOK), BF),
            ((WIDE, KEYS), BF),
            ((KEYS, BLK), F32),
            ((KEYS, BLK), BF),
        ],
        flops=10**10,
    )


def backward(fetch, reads, here, stat):
    return call(
        backward_kernel,
        shape(VIEWS, BACK_ROWS, WIDE),
        (fetch, reads, here, stat),
        smem=2,
        scratch=[
            ((HEAD_DIM, VIEWS * TOK), BF),
            ((HEAD_DIM, KEYS), BF),
            ((KEYS, BLK), BF),
            ((VIEWS, TOK, WIDE), F32),
        ],
        flops=2 * 10**10,
    )


def swap(rows, axis):
    return lax.all_to_all(rows, axis, split_axis=0, concat_axis=0, tiled=True)


def ring_sum(pieces, scene, size, step):
    here = (scene // step) % size
    total = lax.dynamic_index_in_dim(pieces, here, 0, keepdims=False).astype(F32)
    scenes = X * ZHI * CORES
    for d in range(1, size):
        pairs = []
        for i in range(scenes):
            at = (i // step) % size
            pairs.append((i, i + ((at + d) % size - at) * step))
        send = lax.dynamic_index_in_dim(pieces, (here + d) % size, 0, keepdims=False)
        total = total + lax.ppermute(send, "scene", pairs).astype(F32)
    return total.astype(BF)


def on_device(query_rows, key_rows, value_rows, grad_out, out_weight, fetch_list, read_mask):
    go = grad_out[0, 0]
    scene = lax.axis_index("scene")
    fetch = fetch_list.reshape(VIEWS * VIEWS)
    sent = call(
        pack_kernel,
        shape(VIEWS, PACK_ROWS, WIDE),
        (query_rows[0, 0], key_rows[0, 0], value_rows[0, 0], go, out_weight, read_mask[0, 0]),
    )
    here = swap(sent, "view")
    reads = here[:, ROWS, :VIEWS].astype(jnp.int32).reshape(VIEWS * VIEWS)
    attn, stat = forward(fetch, reads, here)
    attn_home = swap(attn, "view")
    back = backward(fetch, reads, here, stat)
    attn_home, back = lax.optimization_barrier((attn_home, back))
    core = (scene % CORES).astype(jnp.int32)[None]
    own = INNER // (X * ZHI * CORES)
    piece = shape(X, ZHI, own, D)
    layer, mine, other = call(
        project_kernel,
        (shape(TOK, D), piece, piece),
        (core, attn_home, go, out_weight),
        smem=1,
        scratch=[((TOK, INNER), BF), ((INNER, D), BF)],
        flops=10**9,
    )
    home = swap(back, "view")
    scenes = X * ZHI * CORES
    other = lax.ppermute(other, "scene", [(i, i ^ 1) for i in range(scenes)])
    term = (mine.astype(F32) + other.astype(F32)).astype(BF)
    term = ring_sum(term, scene, X, ZHI * CORES)
    term = ring_sum(term, scene, ZHI, CORES)
    term, home = lax.optimization_barrier((term, home))
    term = swap(term.reshape(own, VIEWS, COLS).transpose(1, 0, 2), "view")
    share = jnp.sum(term.astype(F32), axis=0) * float(scenes * VIEWS * TOK) ** (-0.5)
    gq, gk, gv = call(unpack_kernel, (shape(TOK, INNER),) * 3, (home,))
    return (layer[None, None], gq[None, None], gk[None, None], gv[None, None], share)


def solution(mesh):
    rows = P("scene", "view", None, None)
    return jax.shard_map(
        on_device,
        mesh=mesh,
        in_specs=(rows, rows, rows, rows, P(), P("scene", None, None), rows),
        out_specs=(rows, rows, rows, rows, P("scene", "view")),
        check_vma=False,
    )
```

```python
import jax
import jax.numpy as jnp
from jax import lax
from jax.experimental import pallas as pl
from jax.experimental.pallas import tpu as pltpu
from jax.sharding import PartitionSpec as P

HEADS = 8
HEAD_DIM = 64
BLK = 128
TOK = 256
VIEWS = 16
INNER = 512
D = 1024
KEYS = TOK + VIEWS * BLK
WIDE = 2 * HEAD_DIM
COLS = D // VIEWS
BF = jnp.bfloat16
F32 = jnp.float32
SCALE = HEAD_DIM ** (-0.5)
ROWS = TOK + BLK
PACK_ROWS = ROWS + 16
CHUNK = 768
BACK_ROWS = TOK + BLK // 2
X, ZHI, CORES = 4, 4, 2
ZLO, Y = 4, 4
NT = (((1,), (1,)), ((), ()))
VMEM = pl.BlockSpec(memory_space=pltpu.VMEM)
SMEM = pl.BlockSpec(memory_space=pltpu.SMEM)


def pack_kernel(q_ref, k_ref, v_ref, go_ref, w_ref, mask_ref, out_ref):
    ga = lax.dot_general(go_ref[...], w_ref[...], NT, preferred_element_type=F32).astype(BF)
    q = q_ref[...] * jnp.asarray(SCALE, BF)
    for h in range(HEADS):
        c = slice(h * HEAD_DIM, (h + 1) * HEAD_DIM)
        kv = jnp.concatenate([k_ref[:, c], v_ref[:, c]], axis=1)
        qg = jnp.concatenate([q[:, c], ga[:, c]], axis=1)
        for p in range(2):
            j = 2 * h + p
            out_ref[j, 0:TOK, :] = kv
            out_ref[j, TOK:ROWS, :] = qg[p * BLK : (p + 1) * BLK, :]
            out_ref[j, ROWS:PACK_ROWS, 0:VIEWS] = jnp.broadcast_to(
                mask_ref[p : p + 1, :], (16, VIEWS)
            ).astype(BF)


def rows_of(v, w, fetch_ref):
    return pl.ds(pl.multiple_of(fetch_ref[v * VIEWS + w] * BLK, BLK), BLK)


def bias_of(v, w, mask_ref):
    seen = jnp.logical_and(mask_ref[v * VIEWS + w] == 1, w != v)
    return jnp.where(seen, 0.0, -jnp.inf)


def gather_cols(v, src, dst, dims, fetch_ref):
    dst[dims, 0:TOK] = src[:, pl.ds(pl.multiple_of(v * TOK, TOK), TOK)]
    for w in range(VIEWS):
        at = pl.multiple_of(w * TOK + fetch_ref[v * VIEWS + w] * BLK, BLK)
        dst[dims, TOK + w * BLK : TOK + (w + 1) * BLK] = src[:, pl.ds(at, BLK)]


def gather_rows(v, in_ref, dst, fetch_ref):
    dst[0:TOK, :] = in_ref[v, 0:TOK, :]
    for w in range(VIEWS):
        dst[TOK + w * BLK : TOK + (w + 1) * BLK, :] = in_ref[w, rows_of(v, w, fetch_ref), :]


def side_by_side(t):
    half = BLK // 2
    return jnp.concatenate([t[:, :half], t[:, half:]], axis=0).T


def forward_kernel(fetch_ref, mask_ref, in_ref, attn_ref, stat_ref, vt, vsel, s_ref, e_ref, top_ref, kall):
    lane = lax.broadcasted_iota(jnp.int32, (BLK, WIDE), 1)
    for w in range(VIEWS):
        vt[:, w * TOK : (w + 1) * TOK] = in_ref[w, 0:TOK, :].T[HEAD_DIM:, :]
    vsel[0:HEAD_DIM, :] = jnp.ones((HEAD_DIM, KEYS), BF)

    def scores(v, slot):
        qg = in_ref[v, TOK:ROWS, :]
        qs = jnp.where(lane < HEAD_DIM, qg, jnp.zeros_like(qg))
        gather_rows(v, in_ref, kall.at[slot], fetch_ref)
        top = None
        for c in range(0, KEYS, CHUNK):
            r = lax.dot_general(
                kall[slot, c : c + CHUNK, :], qs, NT, preferred_element_type=F32
            )
            for b in range(0, CHUNK, BLK):
                s = r[b : b + BLK, :]
                w = (c + b - TOK) // BLK
                if w >= 0:
                    s = s + bias_of(v, w, mask_ref)
                s_ref[slot, c + b : c + b + BLK, :] = s
                best = jnp.max(s.reshape(BLK // 8, 8, BLK), axis=0)
                top = best if top is None else jnp.maximum(top, best)
        top_ref[slot, 0:1, :] = jnp.max(top, axis=0, keepdims=True)

    def output(v, slot):
        qg = in_ref[v, TOK:ROWS, :]
        gather_cols(v, vt, vsel, slice(HEAD_DIM, WIDE), fetch_ref)
        top = top_ref[slot, 0:1, :]
        for c in range(KEYS // BLK):
            rows = slice(c * BLK, (c + 1) * BLK)
            e_ref[slot, rows, :] = jnp.exp(s_ref[slot, rows, :] - top).astype(BF)
        o = jnp.dot(vsel[...], e_ref[slot], preferred_element_type=F32)
        share = 1.0 / o[0:1, :]
        attn = o[HEAD_DIM:, :] * share
        attn_ref[v, :, :] = side_by_side(attn).astype(BF)
        delta = jnp.sum(attn * qg.T[HEAD_DIM:, :].astype(F32), axis=0, keepdims=True)
        stat_ref[v, 0:1, :] = top
        stat_ref[v, 1:2, :] = share
        stat_ref[v, 2:3, :] = delta

    def two_views(i, carry):
        v = 2 * i
        scores(v + 1, 1)
        output(v, 0)
        scores(jnp.minimum(v + 2, VIEWS - 1), 0)
        output(v + 1, 1)
        return carry

    scores(0, 0)
    lax.fori_loop(0, VIEWS // 2, two_views, 0)


def backward_kernel(
    fetch_ref, mask_ref, in_ref, stat_ref, out_ref, kt, ksel, x_ref, acc, kall, qg2_ref
):
    lane = lax.broadcasted_iota(jnp.int32, (BLK, WIDE), 1)
    for w in range(VIEWS):
        kt[:, w * TOK : (w + 1) * TOK] = in_ref[w, 0:TOK, :].T[:HEAD_DIM, :]
        acc[w] = jnp.zeros((TOK, WIDE), F32)

    def weights(v, slot):
        qg = in_ref[v, TOK:ROWS, :]
        zero = jnp.zeros_like(qg)
        qg2_ref[slot, 0:BLK, :] = jnp.where(lane < HEAD_DIM, qg, zero)
        qg2_ref[slot, BLK:, :] = jnp.where(lane >= HEAD_DIM, qg, zero)
        qg2 = qg2_ref[slot]
        top = stat_ref[v, 0:1, :]
        share = stat_ref[v, 1:2, :]
        delta = stat_ref[v, 2:3, :]
        gather_rows(v, in_ref, kall.at[slot], fetch_ref)
        for c in range(0, KEYS, 768):
            r = lax.dot_general(
                kall[slot, c : c + 768, :], qg2, NT, preferred_element_type=F32
            )
            for b in range(0, 768, BLK):
                rows = slice(c + b, c + b + BLK)
                s = r[b : b + BLK, 0:BLK]
                w = (c + b - TOK) // BLK
                if w >= 0:
                    s = s + bias_of(v, w, mask_ref)
                prob = jnp.exp(s - top) * share
                x_ref[slot, rows, 0:BLK] = (prob * (r[b : b + BLK, BLK:] - delta)).astype(BF)
                x_ref[slot, rows, BLK:] = prob.astype(BF)

    def sums(v, slot):
        for c in range(0, KEYS, 768):
            g = jnp.dot(x_ref[slot, c : c + 768, :], qg2_ref[slot], preferred_element_type=F32)
            for b in range(0, 768, BLK):
                w = (c + b - TOK) // BLK
                if w >= 0:
                    acc[w, rows_of(v, w, fetch_ref), :] += g[b : b + BLK, :]
                else:
                    acc[v, c + b : c + b + BLK, :] += g[b : b + BLK, :]
        gather_cols(v, kt, ksel, slice(0, HEAD_DIM), fetch_ref)
        o = jnp.dot(ksel[...], x_ref[slot, :, 0:BLK], preferred_element_type=F32) * SCALE
        out_ref[v, TOK:BACK_ROWS, :] = side_by_side(o).astype(BF)

    def two_views(i, carry):
        v = 2 * i
        weights(v + 1, 1)
        sums(v, 0)
        weights(jnp.minimum(v + 2, VIEWS - 1), 0)
        sums(v + 1, 1)
        return carry

    weights(0, 0)
    lax.fori_loop(0, VIEWS // 2, two_views, 0)
    for w in range(VIEWS):
        out_ref[w, 0:TOK, :] = acc[w].astype(BF)


def project_kernel(core_ref, in_ref, go_ref, w_ref, layer_ref, mine_ref, other_ref, attn, term):
    half = BLK // 2
    for h in range(HEADS):
        c = slice(h * HEAD_DIM, (h + 1) * HEAD_DIM)
        for p in range(2):
            both = in_ref[2 * h + p]
            attn[p * BLK : p * BLK + half, c] = both[:, :HEAD_DIM]
            attn[p * BLK + half : (p + 1) * BLK, c] = both[:, HEAD_DIM:]
    layer_ref[...] = jnp.dot(attn[...], w_ref[...], preferred_element_type=F32).astype(BF)
    cols = [(z * Y + y) * COLS for y in range(Y) for z in range(ZLO)]
    go = jnp.concatenate([go_ref[:, c : c + COLS] for c in cols], axis=1)
    term[...] = lax.dot_general(
        attn[...], go, (((0,), (0,)), ((), ())), preferred_element_type=F32
    ).astype(BF)
    core = core_ref[0]
    own = INNER // (X * ZHI * CORES)
    wide = ZLO * COLS
    for x in range(X):
        for side, ref in ((core, mine_ref), (1 - core, other_ref)):
            for z in range(ZHI):
                at = pl.multiple_of((x * ZHI + z) * CORES * own + side * own, own)
                rows = term[pl.ds(at, own), :]
                for y in range(Y):
                    ref[x, y, z, :, :] = rows[:, y * wide : (y + 1) * wide]


def unpack_kernel(in_ref, gq_ref, gk_ref, gv_ref):
    half = BLK // 2
    for h in range(HEADS):
        c = slice(h * HEAD_DIM, (h + 1) * HEAD_DIM)
        kv = in_ref[2 * h, 0:TOK, :].astype(F32) + in_ref[2 * h + 1, 0:TOK, :].astype(F32)
        kv = kv.astype(BF)
        gk_ref[:, c] = kv[:, :HEAD_DIM]
        gv_ref[:, c] = kv[:, HEAD_DIM:]
        for p in range(2):
            both = in_ref[2 * h + p, TOK:BACK_ROWS, :]
            gq_ref[p * BLK : p * BLK + half, c] = both[:, :HEAD_DIM]
            gq_ref[p * BLK + half : (p + 1) * BLK, c] = both[:, HEAD_DIM:]


def shape(*dims, dtype=BF):
    return jax.ShapeDtypeStruct(dims, dtype)


def call(kernel, outs, args, smem=0, scratch=(), mib=32, flops=0):
    return pl.pallas_call(
        kernel,
        out_shape=outs,
        in_specs=[SMEM] * smem + [VMEM] * (len(args) - smem),
        out_specs=jax.tree.map(lambda _: VMEM, outs),
        scratch_shapes=[pltpu.VMEM(dims, dtype) for dims, dtype in scratch],
        compiler_params=pltpu.CompilerParams(vmem_limit_bytes=mib * 1024 * 1024),
        cost_estimate=pl.CostEstimate(flops=flops, bytes_accessed=4 << 20, transcendentals=0),
    )(*args)


def forward(fetch, reads, here):
    return call(
        forward_kernel,
        (shape(VIEWS, BLK // 2, WIDE), shape(VIEWS, 8, BLK, dtype=F32)),
        (fetch, reads, here),
        smem=2,
        scratch=[
            ((HEAD_DIM, VIEWS * TOK), BF),
            ((WIDE, KEYS), BF),
            ((2, KEYS, BLK), F32),
            ((2, KEYS, BLK), BF),
            ((2, 8, BLK), F32),
            ((2, KEYS, WIDE), BF),
        ],
        flops=10**10,
    )


def backward(fetch, reads, here, stat):
    return call(
        backward_kernel,
        shape(VIEWS, BACK_ROWS, WIDE),
        (fetch, reads, here, stat),
        smem=2,
        scratch=[
            ((HEAD_DIM, VIEWS * TOK), BF),
            ((HEAD_DIM, KEYS), BF),
            ((2, KEYS, 2 * BLK), BF),
            ((VIEWS, TOK, WIDE), F32),
            ((2, KEYS, WIDE), BF),
            ((2, 2 * BLK, WIDE), BF),
        ],
        flops=2 * 10**10,
    )


def swap(rows, axis):
    return lax.all_to_all(rows, axis, split_axis=0, concat_axis=0, tiled=True)


def ring_sum(pieces, axis, count, size, step):
    here = (lax.axis_index(axis) // step) % size
    total = lax.dynamic_index_in_dim(pieces, here, 0, keepdims=False).astype(F32)
    for d in range(1, size):
        pairs = []
        for i in range(count):
            at = (i // step) % size
            pairs.append((i, i + ((at + d) % size - at) * step))
        send = lax.dynamic_index_in_dim(pieces, (here + d) % size, 0, keepdims=False)
        total = total + lax.ppermute(send, axis, pairs).astype(F32)
    return total


def on_device(query_rows, key_rows, value_rows, grad_out, out_weight, fetch_list, read_mask):
    go = grad_out[0, 0]
    fetch = fetch_list.reshape(VIEWS * VIEWS)
    sent = call(
        pack_kernel,
        shape(VIEWS, PACK_ROWS, WIDE),
        (query_rows[0, 0], key_rows[0, 0], value_rows[0, 0], go, out_weight, read_mask[0, 0]),
        mib=60,
    )
    here = swap(sent, "view")
    reads = here[:, ROWS, :VIEWS].astype(jnp.int32).reshape(VIEWS * VIEWS)
    attn, stat = forward(fetch, reads, here)
    attn_home = swap(attn, "view")
    back = backward(fetch, reads, here, stat)
    attn_home, back = lax.optimization_barrier((attn_home, back))
    core = (lax.axis_index("scene") % CORES).astype(jnp.int32)[None]
    own = INNER // (X * ZHI * CORES)
    piece = shape(X, Y, ZHI, own, ZLO * COLS)
    layer, mine, other = call(
        project_kernel,
        (shape(TOK, D), piece, piece),
        (core, attn_home, go, out_weight),
        smem=1,
        scratch=[((TOK, INNER), BF), ((INNER, D), BF)],
        flops=10**9,
    )
    home = swap(back, "view")
    scenes = X * ZHI * CORES
    other = lax.ppermute(other, "scene", [(i, i ^ 1) for i in range(scenes)])
    term = (mine.astype(F32) + other.astype(F32)).astype(BF)
    term = ring_sum(term, "scene", scenes, X, ZHI * CORES).astype(BF)
    term = ring_sum(term, "view", VIEWS, Y, 1).astype(BF)
    term = ring_sum(term, "scene", scenes, ZHI, CORES).astype(BF)
    term = term.reshape(own, ZLO, COLS).transpose(1, 0, 2)
    share = ring_sum(term, "view", VIEWS, ZLO, Y) * float(scenes * VIEWS * TOK) ** (-0.5)
    gq, gk, gv = call(unpack_kernel, (shape(TOK, INNER),) * 3, (home,))
    return (layer[None, None], gq[None, None], gk[None, None], gv[None, None], share)


def solution(mesh):
    rows = P("scene", "view", None, None)
    return jax.shard_map(
        on_device,
        mesh=mesh,
        in_specs=(rows, rows, rows, rows, P(), P("scene", None, None), rows),
        out_specs=(rows, rows, rows, rows, P("scene", "view")),
        check_vma=False,
    )
```

```python
import jax
import jax.numpy as jnp
from jax import lax
from jax.experimental import pallas as pl
from jax.experimental.pallas import tpu as pltpu
from jax.sharding import PartitionSpec as P

HEADS = 8
HEAD_DIM = 64
BLK = 128
TOK = 256
VIEWS = 16
INNER = 512
D = 1024
KEYS = TOK + VIEWS * BLK
WIDE = 2 * HEAD_DIM
COLS = D // VIEWS
BF = jnp.bfloat16
F32 = jnp.float32
SCALE = HEAD_DIM ** (-0.5)
ROWS = TOK + BLK
PACK_ROWS = ROWS + 16
CHUNK = 768
BACK_ROWS = TOK + BLK // 2
X, ZHI, CORES = 4, 4, 2
ZLO, Y = 4, 4
NT = (((1,), (1,)), ((), ()))
VMEM = pl.BlockSpec(memory_space=pltpu.VMEM)
SMEM = pl.BlockSpec(memory_space=pltpu.SMEM)


def pack_kernel(q_ref, k_ref, v_ref, go_ref, w_ref, mask_ref, out_ref):
    ga = lax.dot_general(go_ref[...], w_ref[...], NT, preferred_element_type=F32).astype(BF)
    q = q_ref[...] * jnp.asarray(SCALE, BF)
    for h in range(HEADS):
        c = slice(h * HEAD_DIM, (h + 1) * HEAD_DIM)
        kv = jnp.concatenate([k_ref[:, c], v_ref[:, c]], axis=1)
        qg = jnp.concatenate([q[:, c], ga[:, c]], axis=1)
        for p in range(2):
            j = 2 * h + p
            out_ref[j, 0:TOK, :] = kv
            out_ref[j, TOK:ROWS, :] = qg[p * BLK : (p + 1) * BLK, :]
            out_ref[j, ROWS:PACK_ROWS, 0:VIEWS] = jnp.broadcast_to(
                mask_ref[p : p + 1, :], (16, VIEWS)
            ).astype(BF)


def rows_of(v, w, fetch_ref):
    return pl.ds(pl.multiple_of(fetch_ref[v * VIEWS + w] * BLK, BLK), BLK)


def bias_of(v, w, mask_ref):
    seen = jnp.logical_and(mask_ref[v * VIEWS + w] == 1, w != v)
    return jnp.where(seen, 0.0, -jnp.inf)


def gather_cols(v, src, dst, dims, fetch_ref):
    dst[dims, 0:TOK] = src[:, pl.ds(pl.multiple_of(v * TOK, TOK), TOK)]
    for w in range(VIEWS):
        at = pl.multiple_of(w * TOK + fetch_ref[v * VIEWS + w] * BLK, BLK)
        dst[dims, TOK + w * BLK : TOK + (w + 1) * BLK] = src[:, pl.ds(at, BLK)]


def gather_rows(v, in_ref, dst, fetch_ref):
    dst[0:TOK, :] = in_ref[v, 0:TOK, :]
    for w in range(VIEWS):
        dst[TOK + w * BLK : TOK + (w + 1) * BLK, :] = in_ref[w, rows_of(v, w, fetch_ref), :]


def side_by_side(t):
    half = BLK // 2
    return jnp.concatenate([t[:, :half], t[:, half:]], axis=0).T


def forward_kernel(fetch_ref, mask_ref, in_ref, attn_ref, stat_ref, vt, vsel, s_ref, e_ref, top_ref, kall):
    lane = lax.broadcasted_iota(jnp.int32, (BLK, WIDE), 1)
    for w in range(VIEWS):
        vt[:, w * TOK : (w + 1) * TOK] = in_ref[w, 0:TOK, :].T[HEAD_DIM:, :]
    vsel[0:HEAD_DIM, :] = jnp.ones((HEAD_DIM, KEYS), BF)

    def scores(v, slot):
        qg = in_ref[v, TOK:ROWS, :]
        qs = jnp.where(lane < HEAD_DIM, qg, jnp.zeros_like(qg))
        gather_rows(v, in_ref, kall.at[slot], fetch_ref)
        top = None
        for c in range(0, KEYS, CHUNK):
            r = lax.dot_general(
                kall[slot, c : c + CHUNK, :], qs, NT, preferred_element_type=F32
            )
            for b in range(0, CHUNK, BLK):
                s = r[b : b + BLK, :]
                w = (c + b - TOK) // BLK
                if w >= 0:
                    s = s + bias_of(v, w, mask_ref)
                s_ref[slot, c + b : c + b + BLK, :] = s
                best = jnp.max(s.reshape(BLK // 8, 8, BLK), axis=0)
                top = best if top is None else jnp.maximum(top, best)
        top_ref[slot, 0:1, :] = jnp.max(top, axis=0, keepdims=True)

    def output(v, slot):
        qg = in_ref[v, TOK:ROWS, :]
        gather_cols(v, vt, vsel, slice(HEAD_DIM, WIDE), fetch_ref)
        top = top_ref[slot, 0:1, :]
        for c in range(KEYS // BLK):
            rows = slice(c * BLK, (c + 1) * BLK)
            e_ref[slot, rows, :] = jnp.exp(s_ref[slot, rows, :] - top).astype(BF)
        o = jnp.dot(vsel[...], e_ref[slot], preferred_element_type=F32)
        share = 1.0 / o[0:1, :]
        attn = o[HEAD_DIM:, :] * share
        attn_ref[v, :, :] = side_by_side(attn).astype(BF)
        delta = jnp.sum(attn * qg.T[HEAD_DIM:, :].astype(F32), axis=0, keepdims=True)
        stat_ref[v, 0:1, :] = top
        stat_ref[v, 1:2, :] = share
        stat_ref[v, 2:3, :] = delta

    def two_views(i, carry):
        v = 2 * i
        scores(v + 1, 1)
        output(v, 0)
        scores(jnp.minimum(v + 2, VIEWS - 1), 0)
        output(v + 1, 1)
        return carry

    scores(0, 0)
    lax.fori_loop(0, VIEWS // 2, two_views, 0)


def backward_kernel(
    fetch_ref, mask_ref, in_ref, stat_ref, out_ref, kt, ksel, x_ref, acc, kall, qg2_ref
):
    lane = lax.broadcasted_iota(jnp.int32, (BLK, WIDE), 1)
    for w in range(VIEWS):
        kt[:, w * TOK : (w + 1) * TOK] = in_ref[w, 0:TOK, :].T[:HEAD_DIM, :]
        acc[w] = jnp.zeros((TOK, WIDE), F32)

    def weights(v, slot):
        qg = in_ref[v, TOK:ROWS, :]
        zero = jnp.zeros_like(qg)
        qg2_ref[slot, 0:BLK, :] = jnp.where(lane < HEAD_DIM, qg, zero)
        qg2_ref[slot, BLK:, :] = jnp.where(lane >= HEAD_DIM, qg, zero)
        qg2 = qg2_ref[slot]
        top = stat_ref[v, 0:1, :]
        share = stat_ref[v, 1:2, :]
        delta = stat_ref[v, 2:3, :]
        gather_rows(v, in_ref, kall.at[slot], fetch_ref)
        for c in range(0, KEYS, 768):
            r = lax.dot_general(
                kall[slot, c : c + 768, :], qg2, NT, preferred_element_type=F32
            )
            for b in range(0, 768, BLK):
                rows = slice(c + b, c + b + BLK)
                s = r[b : b + BLK, 0:BLK]
                w = (c + b - TOK) // BLK
                if w >= 0:
                    s = s + bias_of(v, w, mask_ref)
                prob = jnp.exp(s - top) * share
                x_ref[slot, rows, 0:BLK] = (prob * (r[b : b + BLK, BLK:] - delta)).astype(BF)
                x_ref[slot, rows, BLK:] = prob.astype(BF)

    def sums(v, slot):
        for c in range(0, KEYS, 768):
            g = jnp.dot(x_ref[slot, c : c + 768, :], qg2_ref[slot], preferred_element_type=F32)
            for b in range(0, 768, BLK):
                w = (c + b - TOK) // BLK
                if w >= 0:
                    acc[w, rows_of(v, w, fetch_ref), :] += g[b : b + BLK, :]
                else:
                    acc[v, c + b : c + b + BLK, :] += g[b : b + BLK, :]
        gather_cols(v, kt, ksel, slice(0, HEAD_DIM), fetch_ref)
        o = jnp.dot(ksel[...], x_ref[slot, :, 0:BLK], preferred_element_type=F32) * SCALE
        out_ref[v, TOK:BACK_ROWS, :] = side_by_side(o).astype(BF)

    def two_views(i, carry):
        v = 2 * i
        weights(v + 1, 1)
        sums(v, 0)
        weights(jnp.minimum(v + 2, VIEWS - 1), 0)
        sums(v + 1, 1)
        return carry

    weights(0, 0)
    lax.fori_loop(0, VIEWS // 2, two_views, 0)
    for w in range(VIEWS):
        out_ref[w, 0:TOK, :] = acc[w].astype(BF)


def project_kernel(core_ref, in_ref, go_ref, w_ref, layer_ref, mine_ref, other_ref, attn, term):
    half = BLK // 2
    for h in range(HEADS):
        c = slice(h * HEAD_DIM, (h + 1) * HEAD_DIM)
        for p in range(2):
            both = in_ref[2 * h + p]
            attn[p * BLK : p * BLK + half, c] = both[:, :HEAD_DIM]
            attn[p * BLK + half : (p + 1) * BLK, c] = both[:, HEAD_DIM:]
    layer_ref[...] = jnp.dot(attn[...], w_ref[...], preferred_element_type=F32).astype(BF)
    cols = [(z * Y + y) * COLS for y in range(Y) for z in range(ZLO)]
    go = jnp.concatenate([go_ref[:, c : c + COLS] for c in cols], axis=1)
    term[...] = lax.dot_general(
        attn[...], go, (((0,), (0,)), ((), ())), preferred_element_type=F32
    ).astype(BF)
    core = core_ref[0]
    own = INNER // (X * ZHI * CORES)
    wide = ZLO * COLS
    for x in range(X):
        for side, ref in ((core, mine_ref), (1 - core, other_ref)):
            for z in range(ZHI):
                at = pl.multiple_of((x * ZHI + z) * CORES * own + side * own, own)
                rows = term[pl.ds(at, own), :]
                for y in range(Y):
                    ref[x, y, z, :, :] = rows[:, y * wide : (y + 1) * wide]


def unpack_kernel(in_ref, gq_ref, gk_ref, gv_ref):
    half = BLK // 2
    for h in range(HEADS):
        c = slice(h * HEAD_DIM, (h + 1) * HEAD_DIM)
        kv = in_ref[2 * h, 0:TOK, :].astype(F32) + in_ref[2 * h + 1, 0:TOK, :].astype(F32)
        kv = kv.astype(BF)
        gk_ref[:, c] = kv[:, :HEAD_DIM]
        gv_ref[:, c] = kv[:, HEAD_DIM:]
        for p in range(2):
            both = in_ref[2 * h + p, TOK:BACK_ROWS, :]
            gq_ref[p * BLK : p * BLK + half, c] = both[:, :HEAD_DIM]
            gq_ref[p * BLK + half : (p + 1) * BLK, c] = both[:, HEAD_DIM:]


def shape(*dims, dtype=BF):
    return jax.ShapeDtypeStruct(dims, dtype)


def call(kernel, outs, args, smem=0, scratch=(), mib=32, flops=0):
    return pl.pallas_call(
        kernel,
        out_shape=outs,
        in_specs=[SMEM] * smem + [VMEM] * (len(args) - smem),
        out_specs=jax.tree.map(lambda _: VMEM, outs),
        scratch_shapes=[pltpu.VMEM(dims, dtype) for dims, dtype in scratch],
        compiler_params=pltpu.CompilerParams(vmem_limit_bytes=mib * 1024 * 1024),
        cost_estimate=pl.CostEstimate(flops=flops, bytes_accessed=4 << 20, transcendentals=0),
    )(*args)


def forward(fetch, reads, here):
    return call(
        forward_kernel,
        (shape(VIEWS, BLK // 2, WIDE), shape(VIEWS, 8, BLK, dtype=F32)),
        (fetch, reads, here),
        smem=2,
        scratch=[
            ((HEAD_DIM, VIEWS * TOK), BF),
            ((WIDE, KEYS), BF),
            ((2, KEYS, BLK), F32),
            ((2, KEYS, BLK), BF),
            ((2, 8, BLK), F32),
            ((2, KEYS, WIDE), BF),
        ],
        flops=10**10,
    )


def backward(fetch, reads, here, stat):
    return call(
        backward_kernel,
        shape(VIEWS, BACK_ROWS, WIDE),
        (fetch, reads, here, stat),
        smem=2,
        scratch=[
            ((HEAD_DIM, VIEWS * TOK), BF),
            ((HEAD_DIM, KEYS), BF),
            ((2, KEYS, 2 * BLK), BF),
            ((VIEWS, TOK, WIDE), F32),
            ((2, KEYS, WIDE), BF),
            ((2, 2 * BLK, WIDE), BF),
        ],
        flops=2 * 10**10,
    )


def swap(rows, axis):
    return lax.all_to_all(rows, axis, split_axis=0, concat_axis=0, tiled=True)


def ring_sum(pieces, axis, count, size, step):
    here = (lax.axis_index(axis) // step) % size
    total = lax.dynamic_index_in_dim(pieces, here, 0, keepdims=False).astype(F32)
    for d in range(1, size):
        pairs = []
        for i in range(count):
            at = (i // step) % size
            pairs.append((i, i + ((at + d) % size - at) * step))
        send = lax.dynamic_index_in_dim(pieces, (here + d) % size, 0, keepdims=False)
        total = total + lax.ppermute(send, axis, pairs).astype(F32)
    return total


def on_device(query_rows, key_rows, value_rows, grad_out, out_weight, fetch_list, read_mask):
    go = grad_out[0, 0]
    fetch = fetch_list.reshape(VIEWS * VIEWS)
    sent = call(
        pack_kernel,
        shape(VIEWS, PACK_ROWS, WIDE),
        (query_rows[0, 0], key_rows[0, 0], value_rows[0, 0], go, out_weight, read_mask[0, 0]),
        mib=60,
    )
    here = swap(sent, "view")
    reads = here[:, ROWS, :VIEWS].astype(jnp.int32).reshape(VIEWS * VIEWS)
    attn, stat = forward(fetch, reads, here)
    attn_home = swap(attn, "view")
    back = backward(fetch, reads, here, stat)
    attn_home, back = lax.optimization_barrier((attn_home, back))
    core = (lax.axis_index("scene") % CORES).astype(jnp.int32)[None]
    own = INNER // (X * ZHI * CORES)
    piece = shape(X, Y, ZHI, own, ZLO * COLS)
    layer, mine, other = call(
        project_kernel,
        (shape(TOK, D), piece, piece),
        (core, attn_home, go, out_weight),
        smem=1,
        scratch=[((TOK, INNER), BF), ((INNER, D), BF)],
        flops=10**9,
    )
    home = swap(back, "view")
    scenes = X * ZHI * CORES
    other = lax.ppermute(other, "scene", [(i, i ^ 1) for i in range(scenes)])
    term = (mine.astype(F32) + other.astype(F32)).astype(BF)
    term = ring_sum(term, "scene", scenes, X, ZHI * CORES).astype(BF)
    term = ring_sum(term, "view", VIEWS, Y, 1).astype(BF)
    term, home = lax.optimization_barrier((term, home))
    term = term.reshape(ZHI, own, ZLO, COLS).transpose(0, 2, 1, 3).reshape(ZHI * ZLO, own, COLS)
    along_z = [
        [((x * ZHI + zh) * CORES + k) * VIEWS + zl * Y + y for zh in range(ZHI) for zl in range(ZLO)]
        for x in range(X)
        for k in range(CORES)
        for y in range(Y)
    ]
    term = lax.all_to_all(
        term, ("scene", "view"), 0, 0, tiled=True, axis_index_groups=along_z
    )
    share = jnp.sum(term.astype(F32), axis=0) * float(scenes * VIEWS * TOK) ** (-0.5)
    gq, gk, gv = call(unpack_kernel, (shape(TOK, INNER),) * 3, (home,))
    return (layer[None, None], gq[None, None], gk[None, None], gv[None, None], share)


def solution(mesh):
    rows = P("scene", "view", None, None)
    return jax.shard_map(
        on_device,
        mesh=mesh,
        in_specs=(rows, rows, rows, rows, P(), P("scene", None, None), rows),
        out_specs=(rows, rows, rows, rows, P("scene", "view")),
        check_vma=False,
    )
```

```python
import jax
import jax.numpy as jnp
from jax import lax
from jax.experimental import pallas as pl
from jax.experimental.pallas import tpu as pltpu
from jax.sharding import PartitionSpec as P

HEADS = 8
HEAD_DIM = 64
BLK = 128
TOK = 256
VIEWS = 16
INNER = 512
D = 1024
KEYS = TOK + VIEWS * BLK
WIDE = 2 * HEAD_DIM
COLS = D // VIEWS
BF = jnp.bfloat16
F32 = jnp.float32
SCALE = HEAD_DIM ** (-0.5)
ROWS = TOK + BLK
PACK_ROWS = ROWS + 16
CHUNK = 768
BACK_ROWS = TOK + BLK // 2
X, ZHI, CORES = 4, 4, 2
ZLO, Y = 4, 4
RING = (0, 2, 3, 1)
NT = (((1,), (1,)), ((), ()))
VMEM = pl.BlockSpec(memory_space=pltpu.VMEM)
SMEM = pl.BlockSpec(memory_space=pltpu.SMEM)


def pack_kernel(q_ref, k_ref, v_ref, go_ref, w_ref, mask_ref, out_ref):
    ga = lax.dot_general(go_ref[...], w_ref[...], NT, preferred_element_type=F32).astype(BF)
    q = q_ref[...] * jnp.asarray(SCALE, BF)
    for h in range(HEADS):
        c = slice(h * HEAD_DIM, (h + 1) * HEAD_DIM)
        kv = jnp.concatenate([k_ref[:, c], v_ref[:, c]], axis=1)
        qg = jnp.concatenate([q[:, c], ga[:, c]], axis=1)
        for p in range(2):
            j = 2 * h + p
            out_ref[j, 0:TOK, :] = kv
            out_ref[j, TOK:ROWS, :] = qg[p * BLK : (p + 1) * BLK, :]
            out_ref[j, ROWS:PACK_ROWS, 0:VIEWS] = jnp.broadcast_to(
                mask_ref[p : p + 1, :], (16, VIEWS)
            ).astype(BF)


def rows_of(v, w, fetch_ref):
    return pl.ds(pl.multiple_of(fetch_ref[v * VIEWS + w] * BLK, BLK), BLK)


def bias_of(v, w, mask_ref):
    seen = jnp.logical_and(mask_ref[v * VIEWS + w] == 1, w != v)
    return jnp.where(seen, 0.0, -jnp.inf)


def gather_cols(v, src, dst, dims, fetch_ref):
    dst[dims, 0:TOK] = src[:, pl.ds(pl.multiple_of(v * TOK, TOK), TOK)]
    for w in range(VIEWS):
        at = pl.multiple_of(w * TOK + fetch_ref[v * VIEWS + w] * BLK, BLK)
        dst[dims, TOK + w * BLK : TOK + (w + 1) * BLK] = src[:, pl.ds(at, BLK)]


def gather_rows(v, in_ref, dst, fetch_ref):
    dst[0:TOK, :] = in_ref[v, 0:TOK, :]
    for w in range(VIEWS):
        dst[TOK + w * BLK : TOK + (w + 1) * BLK, :] = in_ref[w, rows_of(v, w, fetch_ref), :]


def side_by_side(t):
    half = BLK // 2
    return jnp.concatenate([t[:, :half], t[:, half:]], axis=0).T


def forward_kernel(fetch_ref, mask_ref, in_ref, attn_ref, stat_ref, vt, vsel, s_ref, e_ref, top_ref, kall):
    lane = lax.broadcasted_iota(jnp.int32, (BLK, WIDE), 1)
    for w in range(VIEWS):
        vt[:, w * TOK : (w + 1) * TOK] = in_ref[w, 0:TOK, :].T[HEAD_DIM:, :]
    vsel[0:HEAD_DIM, :] = jnp.ones((HEAD_DIM, KEYS), BF)

    def scores(v, slot):
        qg = in_ref[v, TOK:ROWS, :]
        qs = jnp.where(lane < HEAD_DIM, qg, jnp.zeros_like(qg))
        gather_rows(v, in_ref, kall.at[slot], fetch_ref)
        top = None
        for c in range(0, KEYS, CHUNK):
            r = lax.dot_general(
                kall[slot, c : c + CHUNK, :], qs, NT, preferred_element_type=F32
            )
            for b in range(0, CHUNK, BLK):
                s = r[b : b + BLK, :]
                w = (c + b - TOK) // BLK
                if w >= 0:
                    s = s + bias_of(v, w, mask_ref)
                s_ref[slot, c + b : c + b + BLK, :] = s
                best = jnp.max(s.reshape(BLK // 8, 8, BLK), axis=0)
                top = best if top is None else jnp.maximum(top, best)
        top_ref[slot, 0:1, :] = jnp.max(top, axis=0, keepdims=True)

    def output(v, slot):
        qg = in_ref[v, TOK:ROWS, :]
        gather_cols(v, vt, vsel, slice(HEAD_DIM, WIDE), fetch_ref)
        top = top_ref[slot, 0:1, :]
        for c in range(KEYS // BLK):
            rows = slice(c * BLK, (c + 1) * BLK)
            e_ref[slot, rows, :] = jnp.exp(s_ref[slot, rows, :] - top).astype(BF)
        o = jnp.dot(vsel[...], e_ref[slot], preferred_element_type=F32)
        share = 1.0 / o[0:1, :]
        attn = o[HEAD_DIM:, :] * share
        attn_ref[v, :, :] = side_by_side(attn).astype(BF)
        delta = jnp.sum(attn * qg.T[HEAD_DIM:, :].astype(F32), axis=0, keepdims=True)
        stat_ref[v, 0:1, :] = top
        stat_ref[v, 1:2, :] = share
        stat_ref[v, 2:3, :] = delta

    def two_views(i, carry):
        v = 2 * i
        scores(v + 1, 1)
        output(v, 0)
        scores(jnp.minimum(v + 2, VIEWS - 1), 0)
        output(v + 1, 1)
        return carry

    scores(0, 0)
    lax.fori_loop(0, VIEWS // 2, two_views, 0)


def backward_kernel(
    fetch_ref, mask_ref, in_ref, stat_ref, out_ref, kt, ksel, x_ref, acc, kall, qg2_ref
):
    lane = lax.broadcasted_iota(jnp.int32, (BLK, WIDE), 1)
    for w in range(VIEWS):
        kt[:, w * TOK : (w + 1) * TOK] = in_ref[w, 0:TOK, :].T[:HEAD_DIM, :]
        acc[w] = jnp.zeros((TOK, WIDE), F32)

    def weights(v, slot):
        qg = in_ref[v, TOK:ROWS, :]
        zero = jnp.zeros_like(qg)
        qg2_ref[slot, 0:BLK, :] = jnp.where(lane < HEAD_DIM, qg, zero)
        qg2_ref[slot, BLK:, :] = jnp.where(lane >= HEAD_DIM, qg, zero)
        qg2 = qg2_ref[slot]
        top = stat_ref[v, 0:1, :]
        share = stat_ref[v, 1:2, :]
        delta = stat_ref[v, 2:3, :]
        gather_rows(v, in_ref, kall.at[slot], fetch_ref)
        for c in range(0, KEYS, 768):
            r = lax.dot_general(
                kall[slot, c : c + 768, :], qg2, NT, preferred_element_type=F32
            )
            for b in range(0, 768, BLK):
                rows = slice(c + b, c + b + BLK)
                s = r[b : b + BLK, 0:BLK]
                w = (c + b - TOK) // BLK
                if w >= 0:
                    s = s + bias_of(v, w, mask_ref)
                prob = jnp.exp(s - top) * share
                x_ref[slot, rows, 0:BLK] = (prob * (r[b : b + BLK, BLK:] - delta)).astype(BF)
                x_ref[slot, rows, BLK:] = prob.astype(BF)

    def sums(v, slot):
        for c in range(0, KEYS, 768):
            g = jnp.dot(x_ref[slot, c : c + 768, :], qg2_ref[slot], preferred_element_type=F32)
            for b in range(0, 768, BLK):
                w = (c + b - TOK) // BLK
                if w >= 0:
                    acc[w, rows_of(v, w, fetch_ref), :] += g[b : b + BLK, :]
                else:
                    acc[v, c + b : c + b + BLK, :] += g[b : b + BLK, :]
        gather_cols(v, kt, ksel, slice(0, HEAD_DIM), fetch_ref)
        o = jnp.dot(ksel[...], x_ref[slot, :, 0:BLK], preferred_element_type=F32) * SCALE
        out_ref[v, TOK:BACK_ROWS, :] = side_by_side(o).astype(BF)

    def two_views(i, carry):
        v = 2 * i
        weights(v + 1, 1)
        sums(v, 0)
        weights(jnp.minimum(v + 2, VIEWS - 1), 0)
        sums(v + 1, 1)
        return carry

    weights(0, 0)
    lax.fori_loop(0, VIEWS // 2, two_views, 0)
    for w in range(VIEWS):
        out_ref[w, 0:TOK, :] = acc[w].astype(BF)


def project_kernel(core_ref, in_ref, go_ref, w_ref, layer_ref, mine_ref, other_ref, attn, term):
    half = BLK // 2
    for h in range(HEADS):
        c = slice(h * HEAD_DIM, (h + 1) * HEAD_DIM)
        for p in range(2):
            both = in_ref[2 * h + p]
            attn[p * BLK : p * BLK + half, c] = both[:, :HEAD_DIM]
            attn[p * BLK + half : (p + 1) * BLK, c] = both[:, HEAD_DIM:]
    layer_ref[...] = jnp.dot(attn[...], w_ref[...], preferred_element_type=F32).astype(BF)
    cols = [(z * Y + y) * COLS for y in range(Y) for z in range(ZLO)]
    go = jnp.concatenate([go_ref[:, c : c + COLS] for c in cols], axis=1)
    term[...] = lax.dot_general(
        attn[...], go, (((0,), (0,)), ((), ())), preferred_element_type=F32
    ).astype(BF)
    core = core_ref[0]
    own = INNER // (X * ZHI * CORES)
    wide = ZLO * COLS
    for x in range(X):
        for side, ref in ((core, mine_ref), (1 - core, other_ref)):
            for z in range(ZHI):
                at = pl.multiple_of((x * ZHI + z) * CORES * own + side * own, own)
                rows = term[pl.ds(at, own), :]
                for y in range(Y):
                    ref[RING[x], RING[y], z, :, :] = rows[:, y * wide : (y + 1) * wide]


def unpack_kernel(in_ref, gq_ref, gk_ref, gv_ref):
    half = BLK // 2
    for h in range(HEADS):
        c = slice(h * HEAD_DIM, (h + 1) * HEAD_DIM)
        kv = in_ref[2 * h, 0:TOK, :].astype(F32) + in_ref[2 * h + 1, 0:TOK, :].astype(F32)
        kv = kv.astype(BF)
        gk_ref[:, c] = kv[:, :HEAD_DIM]
        gv_ref[:, c] = kv[:, HEAD_DIM:]
        for p in range(2):
            both = in_ref[2 * h + p, TOK:BACK_ROWS, :]
            gq_ref[p * BLK : p * BLK + half, c] = both[:, :HEAD_DIM]
            gq_ref[p * BLK + half : (p + 1) * BLK, c] = both[:, HEAD_DIM:]


def shape(*dims, dtype=BF):
    return jax.ShapeDtypeStruct(dims, dtype)


def call(kernel, outs, args, smem=0, scratch=(), mib=20, flops=0):
    return pl.pallas_call(
        kernel,
        out_shape=outs,
        in_specs=[SMEM] * smem + [VMEM] * (len(args) - smem),
        out_specs=jax.tree.map(lambda _: VMEM, outs),
        scratch_shapes=[pltpu.VMEM(dims, dtype) for dims, dtype in scratch],
        compiler_params=pltpu.CompilerParams(vmem_limit_bytes=mib * 1024 * 1024),
        cost_estimate=pl.CostEstimate(flops=flops, bytes_accessed=4 << 20, transcendentals=0),
    )(*args)


def forward(fetch, reads, here):
    return call(
        forward_kernel,
        (shape(VIEWS, BLK // 2, WIDE), shape(VIEWS, 8, BLK, dtype=F32)),
        (fetch, reads, here),
        smem=2,
        scratch=[
            ((HEAD_DIM, VIEWS * TOK), BF),
            ((WIDE, KEYS), BF),
            ((2, KEYS, BLK), F32),
            ((2, KEYS, BLK), BF),
            ((2, 8, BLK), F32),
            ((2, KEYS, WIDE), BF),
        ],
        flops=10**10,
    )


def backward(fetch, reads, here, stat):
    return call(
        backward_kernel,
        shape(VIEWS, BACK_ROWS, WIDE),
        (fetch, reads, here, stat),
        smem=2,
        scratch=[
            ((HEAD_DIM, VIEWS * TOK), BF),
            ((HEAD_DIM, KEYS), BF),
            ((2, KEYS, 2 * BLK), BF),
            ((VIEWS, TOK, WIDE), F32),
            ((2, KEYS, WIDE), BF),
            ((2, 2 * BLK, WIDE), BF),
        ],
        flops=2 * 10**10,
    )


def swap(rows, axis):
    return lax.all_to_all(rows, axis, split_axis=0, concat_axis=0, tiled=True)


def pair_sums(pieces, axis, count, step):
    here = (lax.axis_index(axis) // step) % 4
    pieces = pieces.reshape((2, 2) + pieces.shape[1:])
    for side, partner in ((((here + 1) // 2) % 2, (1, 0, 3, 2)), (here // 2, (3, 2, 1, 0))):
        pairs = []
        for i in range(count):
            at = (i // step) % 4
            pairs.append((i, i + (partner[at] - at) * step))
        keep = lax.dynamic_index_in_dim(pieces, side, 0, keepdims=False)
        send = lax.dynamic_index_in_dim(pieces, 1 - side, 0, keepdims=False)
        got = lax.ppermute(send, axis, pairs)
        pieces = (keep.astype(F32) + got.astype(F32)).astype(BF)
    return pieces


def on_device(query_rows, key_rows, value_rows, grad_out, out_weight, fetch_list, read_mask):
    go = grad_out[0, 0]
    fetch = fetch_list.reshape(VIEWS * VIEWS)
    sent = call(
        pack_kernel,
        shape(VIEWS, PACK_ROWS, WIDE),
        (query_rows[0, 0], key_rows[0, 0], value_rows[0, 0], go, out_weight, read_mask[0, 0]),
        mib=60,
    )
    here = swap(sent, "view")
    reads = here[:, ROWS, :VIEWS].astype(jnp.int32).reshape(VIEWS * VIEWS)
    attn, stat = forward(fetch, reads, here)
    attn_home = swap(attn, "view")
    back = backward(fetch, reads, here, stat)
    attn_home, back = lax.optimization_barrier((attn_home, back))
    core = (lax.axis_index("scene") % CORES).astype(jnp.int32)[None]
    own = INNER // (X * ZHI * CORES)
    piece = shape(X, Y, ZHI, own, ZLO * COLS)
    layer, mine, other = call(
        project_kernel,
        (shape(TOK, D), piece, piece),
        (core, attn_home, go, out_weight),
        smem=1,
        scratch=[((TOK, INNER), BF), ((INNER, D), BF)],
        flops=10**9,
    )
    home = swap(back, "view")
    scenes = X * ZHI * CORES
    other = lax.ppermute(other, "scene", [(i, i ^ 1) for i in range(scenes)])
    term = (mine.astype(F32) + other.astype(F32)).astype(BF)
    term = pair_sums(term, "scene", scenes, ZHI * CORES)
    term = pair_sums(term, "view", VIEWS, 1)
    term, home = lax.optimization_barrier((term, home))
    term = term.reshape(ZHI, own, ZLO, COLS).transpose(0, 2, 1, 3).reshape(ZHI * ZLO, own, COLS)
    along_z = [
        [((x * ZHI + zh) * CORES + k) * VIEWS + zl * Y + y for zh in range(ZHI) for zl in range(ZLO)]
        for x in range(X)
        for k in range(CORES)
        for y in range(Y)
    ]
    term = lax.all_to_all(
        term, ("scene", "view"), 0, 0, tiled=True, axis_index_groups=along_z
    )
    share = jnp.sum(term.astype(F32), axis=0) * float(scenes * VIEWS * TOK) ** (-0.5)
    gq, gk, gv = call(unpack_kernel, (shape(TOK, INNER),) * 3, (home,))
    return (layer[None, None], gq[None, None], gk[None, None], gv[None, None], share)


def solution(mesh):
    rows = P("scene", "view", None, None)
    return jax.shard_map(
        on_device,
        mesh=mesh,
        in_specs=(rows, rows, rows, rows, P(), P("scene", None, None), rows),
        out_specs=(rows, rows, rows, rows, P("scene", "view")),
        check_vma=False,
    )
```

```python
import jax
import jax.numpy as jnp
from jax import lax
from jax.experimental import pallas as pl
from jax.experimental.pallas import tpu as pltpu
from jax.sharding import PartitionSpec as P

HEADS = 8
HEAD_DIM = 64
BLK = 128
TOK = 256
VIEWS = 16
INNER = 512
D = 1024
KEYS = TOK + VIEWS * BLK
WIDE = 2 * HEAD_DIM
COLS = D // VIEWS
BF = jnp.bfloat16
F32 = jnp.float32
SCALE = HEAD_DIM ** (-0.5)
ROWS = TOK + BLK
PACK_ROWS = ROWS + 16
CHUNK = 768
BACK_ROWS = TOK + BLK // 2
X, ZHI, CORES = 4, 4, 2
ZLO, Y = 4, 4
NT = (((1,), (1,)), ((), ()))
VMEM = pl.BlockSpec(memory_space=pltpu.VMEM)
SMEM = pl.BlockSpec(memory_space=pltpu.SMEM)


def pack_kernel(q_ref, k_ref, v_ref, go_ref, w_ref, mask_ref, out_ref):
    ga = lax.dot_general(go_ref[...], w_ref[...], NT, preferred_element_type=F32).astype(BF)
    q = q_ref[...] * jnp.asarray(SCALE, BF)
    for h in range(HEADS):
        c = slice(h * HEAD_DIM, (h + 1) * HEAD_DIM)
        kv = jnp.concatenate([k_ref[:, c], v_ref[:, c]], axis=1)
        qg = jnp.concatenate([q[:, c], ga[:, c]], axis=1)
        for p in range(2):
            j = 2 * h + p
            out_ref[j, 0:TOK, :] = kv
            out_ref[j, TOK:ROWS, :] = qg[p * BLK : (p + 1) * BLK, :]
            out_ref[j, ROWS:PACK_ROWS, 0:VIEWS] = jnp.broadcast_to(
                mask_ref[p : p + 1, :], (16, VIEWS)
            ).astype(BF)


def rows_of(v, w, fetch_ref):
    return pl.ds(pl.multiple_of(fetch_ref[v * VIEWS + w] * BLK, BLK), BLK)


def bias_of(v, w, mask_ref):
    seen = jnp.logical_and(mask_ref[v * VIEWS + w] == 1, w != v)
    return jnp.where(seen, 0.0, -jnp.inf)


def gather_cols(v, src, dst, dims, fetch_ref):
    dst[dims, 0:TOK] = src[:, pl.ds(pl.multiple_of(v * TOK, TOK), TOK)]
    for w in range(VIEWS):
        at = pl.multiple_of(w * TOK + fetch_ref[v * VIEWS + w] * BLK, BLK)
        dst[dims, TOK + w * BLK : TOK + (w + 1) * BLK] = src[:, pl.ds(at, BLK)]


def gather_rows(v, in_ref, dst, fetch_ref):
    dst[0:TOK, :] = in_ref[v, 0:TOK, :]
    for w in range(VIEWS):
        dst[TOK + w * BLK : TOK + (w + 1) * BLK, :] = in_ref[w, rows_of(v, w, fetch_ref), :]


def side_by_side(t):
    half = BLK // 2
    return jnp.concatenate([t[:, :half], t[:, half:]], axis=0).T


def forward_kernel(fetch_ref, mask_ref, in_ref, attn_ref, stat_ref, vt, vsel, s_ref, e_ref, top_ref, kall):
    lane = lax.broadcasted_iota(jnp.int32, (BLK, WIDE), 1)
    for w in range(VIEWS):
        vt[:, w * TOK : (w + 1) * TOK] = in_ref[w, 0:TOK, :].T[HEAD_DIM:, :]
    vsel[0:HEAD_DIM, :] = jnp.ones((HEAD_DIM, KEYS), BF)

    def scores(v, slot):
        qg = in_ref[v, TOK:ROWS, :]
        qs = jnp.where(lane < HEAD_DIM, qg, jnp.zeros_like(qg))
        gather_rows(v, in_ref, kall.at[slot], fetch_ref)
        top = None
        for c in range(0, KEYS, CHUNK):
            r = lax.dot_general(
                kall[slot, c : c + CHUNK, :], qs, NT, preferred_element_type=F32
            )
            for b in range(0, CHUNK, BLK):
                s = r[b : b + BLK, :]
                w = (c + b - TOK) // BLK
                if w >= 0:
                    s = s + bias_of(v, w, mask_ref)
                s_ref[slot, c + b : c + b + BLK, :] = s
                best = jnp.max(s.reshape(BLK // 8, 8, BLK), axis=0)
                top = best if top is None else jnp.maximum(top, best)
        top_ref[slot, 0:1, :] = jnp.max(top, axis=0, keepdims=True)

    def output(v, slot):
        qg = in_ref[v, TOK:ROWS, :]
        gather_cols(v, vt, vsel, slice(HEAD_DIM, WIDE), fetch_ref)
        top = top_ref[slot, 0:1, :]
        for c in range(KEYS // BLK):
            rows = slice(c * BLK, (c + 1) * BLK)
            e_ref[slot, rows, :] = jnp.exp(s_ref[slot, rows, :] - top).astype(BF)
        o = jnp.dot(vsel[...], e_ref[slot], preferred_element_type=F32)
        share = 1.0 / o[0:1, :]
        attn = o[HEAD_DIM:, :] * share
        attn_ref[v, :, :] = side_by_side(attn).astype(BF)
        delta = jnp.sum(attn * qg.T[HEAD_DIM:, :].astype(F32), axis=0, keepdims=True)
        stat_ref[v, 0:1, :] = top
        stat_ref[v, 1:2, :] = share
        stat_ref[v, 2:3, :] = delta

    def two_views(i, carry):
        v = 2 * i
        scores(v + 1, 1)
        output(v, 0)
        scores(jnp.minimum(v + 2, VIEWS - 1), 0)
        output(v + 1, 1)
        return carry

    scores(0, 0)
    lax.fori_loop(0, VIEWS // 2, two_views, 0)


def backward_kernel(
    fetch_ref, mask_ref, in_ref, stat_ref, out_ref, kt, ksel, x_ref, acc, kall, qg2_ref
):
    lane = lax.broadcasted_iota(jnp.int32, (BLK, WIDE), 1)
    for w in range(VIEWS):
        kt[:, w * TOK : (w + 1) * TOK] = in_ref[w, 0:TOK, :].T[:HEAD_DIM, :]
        acc[w] = jnp.zeros((TOK, WIDE), F32)

    def weights(v, slot):
        qg = in_ref[v, TOK:ROWS, :]
        zero = jnp.zeros_like(qg)
        qg2_ref[slot, 0:BLK, :] = jnp.where(lane < HEAD_DIM, qg, zero)
        qg2_ref[slot, BLK:, :] = jnp.where(lane >= HEAD_DIM, qg, zero)
        qg2 = qg2_ref[slot]
        top = stat_ref[v, 0:1, :]
        share = stat_ref[v, 1:2, :]
        delta = stat_ref[v, 2:3, :]
        gather_rows(v, in_ref, kall.at[slot], fetch_ref)
        for c in range(0, KEYS, 768):
            r = lax.dot_general(
                kall[slot, c : c + 768, :], qg2, NT, preferred_element_type=F32
            )
            for b in range(0, 768, BLK):
                rows = slice(c + b, c + b + BLK)
                s = r[b : b + BLK, 0:BLK]
                w = (c + b - TOK) // BLK
                if w >= 0:
                    s = s + bias_of(v, w, mask_ref)
                prob = jnp.exp(s - top) * share
                x_ref[slot, rows, 0:BLK] = (prob * (r[b : b + BLK, BLK:] - delta)).astype(BF)
                x_ref[slot, rows, BLK:] = prob.astype(BF)

    def sums(v, slot):
        for c in range(0, KEYS, 768):
            g = jnp.dot(x_ref[slot, c : c + 768, :], qg2_ref[slot], preferred_element_type=F32)
            for b in range(0, 768, BLK):
                w = (c + b - TOK) // BLK
                if w >= 0:
                    acc[w, rows_of(v, w, fetch_ref), :] += g[b : b + BLK, :]
                else:
                    acc[v, c + b : c + b + BLK, :] += g[b : b + BLK, :]
        gather_cols(v, kt, ksel, slice(0, HEAD_DIM), fetch_ref)
        o = jnp.dot(ksel[...], x_ref[slot, :, 0:BLK], preferred_element_type=F32) * SCALE
        out_ref[v, TOK:BACK_ROWS, :] = side_by_side(o).astype(BF)

    def two_views(i, carry):
        v = 2 * i
        weights(v + 1, 1)
        sums(v, 0)
        weights(jnp.minimum(v + 2, VIEWS - 1), 0)
        sums(v + 1, 1)
        return carry

    weights(0, 0)
    lax.fori_loop(0, VIEWS // 2, two_views, 0)
    for w in range(VIEWS):
        out_ref[w, 0:TOK, :] = acc[w].astype(BF)


def project_kernel(core_ref, in_ref, go_ref, w_ref, layer_ref, mine_ref, other_ref, attn, term):
    half = BLK // 2
    for h in range(HEADS):
        c = slice(h * HEAD_DIM, (h + 1) * HEAD_DIM)
        for p in range(2):
            both = in_ref[2 * h + p]
            attn[p * BLK : p * BLK + half, c] = both[:, :HEAD_DIM]
            attn[p * BLK + half : (p + 1) * BLK, c] = both[:, HEAD_DIM:]
    layer_ref[...] = jnp.dot(attn[...], w_ref[...], preferred_element_type=F32).astype(BF)
    cols = [(z * Y + y) * COLS for y in range(Y) for z in range(ZLO)]
    go = jnp.concatenate([go_ref[:, c : c + COLS] for c in cols], axis=1)
    term[...] = lax.dot_general(
        attn[...], go, (((0,), (0,)), ((), ())), preferred_element_type=F32
    ).astype(BF)
    core = core_ref[0]
    own = INNER // (X * ZHI * CORES)
    wide = ZLO * COLS
    for x in range(X):
        for side, ref in ((core, mine_ref), (1 - core, other_ref)):
            for z in range(ZHI):
                at = pl.multiple_of((x * ZHI + z) * CORES * own + side * own, own)
                rows = term[pl.ds(at, own), :]
                for y in range(Y):
                    ref[x, y, z, :, :] = rows[:, y * wide : (y + 1) * wide]


def unpack_kernel(in_ref, gq_ref, gk_ref, gv_ref):
    half = BLK // 2
    for h in range(HEADS):
        c = slice(h * HEAD_DIM, (h + 1) * HEAD_DIM)
        kv = in_ref[2 * h, 0:TOK, :].astype(F32) + in_ref[2 * h + 1, 0:TOK, :].astype(F32)
        kv = kv.astype(BF)
        gk_ref[:, c] = kv[:, :HEAD_DIM]
        gv_ref[:, c] = kv[:, HEAD_DIM:]
        for p in range(2):
            both = in_ref[2 * h + p, TOK:BACK_ROWS, :]
            gq_ref[p * BLK : p * BLK + half, c] = both[:, :HEAD_DIM]
            gq_ref[p * BLK + half : (p + 1) * BLK, c] = both[:, HEAD_DIM:]


def shape(*dims, dtype=BF):
    return jax.ShapeDtypeStruct(dims, dtype)


def call(kernel, outs, args, smem=0, scratch=(), mib=32, flops=0):
    return pl.pallas_call(
        kernel,
        out_shape=outs,
        in_specs=[SMEM] * smem + [VMEM] * (len(args) - smem),
        out_specs=jax.tree.map(lambda _: VMEM, outs),
        scratch_shapes=[pltpu.VMEM(dims, dtype) for dims, dtype in scratch],
        compiler_params=pltpu.CompilerParams(vmem_limit_bytes=mib * 1024 * 1024),
        cost_estimate=pl.CostEstimate(flops=flops, bytes_accessed=4 << 20, transcendentals=0),
    )(*args)


def forward(fetch, reads, here):
    return call(
        forward_kernel,
        (shape(VIEWS, BLK // 2, WIDE), shape(VIEWS, 8, BLK, dtype=F32)),
        (fetch, reads, here),
        smem=2,
        scratch=[
            ((HEAD_DIM, VIEWS * TOK), BF),
            ((WIDE, KEYS), BF),
            ((2, KEYS, BLK), F32),
            ((2, KEYS, BLK), BF),
            ((2, 8, BLK), F32),
            ((2, KEYS, WIDE), BF),
        ],
        flops=10**10,
    )


def backward(fetch, reads, here, stat):
    return call(
        backward_kernel,
        shape(VIEWS, BACK_ROWS, WIDE),
        (fetch, reads, here, stat),
        smem=2,
        scratch=[
            ((HEAD_DIM, VIEWS * TOK), BF),
            ((HEAD_DIM, KEYS), BF),
            ((2, KEYS, 2 * BLK), BF),
            ((VIEWS, TOK, WIDE), F32),
            ((2, KEYS, WIDE), BF),
            ((2, 2 * BLK, WIDE), BF),
        ],
        flops=2 * 10**10,
    )


def swap(rows, axis):
    return lax.all_to_all(rows, axis, split_axis=0, concat_axis=0, tiled=True)


def ring_sum(pieces, axis, count, size, step):
    here = (lax.axis_index(axis) // step) % size
    total = lax.dynamic_index_in_dim(pieces, here, 0, keepdims=False).astype(F32)
    for d in range(1, size):
        pairs = []
        for i in range(count):
            at = (i // step) % size
            pairs.append((i, i + ((at + d) % size - at) * step))
        send = lax.dynamic_index_in_dim(pieces, (here + d) % size, 0, keepdims=False)
        total = total + lax.ppermute(send, axis, pairs).astype(F32)
    return total


def on_device(query_rows, key_rows, value_rows, grad_out, out_weight, fetch_list, read_mask):
    go = grad_out[0, 0]
    fetch = fetch_list.reshape(VIEWS * VIEWS)
    sent = call(
        pack_kernel,
        shape(VIEWS, PACK_ROWS, WIDE),
        (query_rows[0, 0], key_rows[0, 0], value_rows[0, 0], go, out_weight, read_mask[0, 0]),
        mib=60,
    )
    here = swap(sent, "view")
    reads = here[:, ROWS, :VIEWS].astype(jnp.int32).reshape(VIEWS * VIEWS)
    attn, stat = forward(fetch, reads, here)
    attn_home = swap(attn, "view")
    back = backward(fetch, reads, here, stat)
    attn_home, back = lax.optimization_barrier((attn_home, back))
    core = (lax.axis_index("scene") % CORES).astype(jnp.int32)[None]
    own = INNER // (X * ZHI * CORES)
    piece = shape(X, Y, ZHI, own, ZLO * COLS)
    layer, mine, other = call(
        project_kernel,
        (shape(TOK, D), piece, piece),
        (core, attn_home, go, out_weight),
        smem=1,
        scratch=[((TOK, INNER), BF), ((INNER, D), BF)],
        flops=10**9,
    )
    home = swap(back, "view")
    scenes = X * ZHI * CORES
    other = lax.ppermute(other, "scene", [(i, i ^ 1) for i in range(scenes)])
    term = (mine.astype(F32) + other.astype(F32)).astype(BF)
    term = ring_sum(term, "scene", scenes, X, ZHI * CORES).astype(BF)
    term = ring_sum(term, "view", VIEWS, Y, 1).astype(BF)
    term, home = lax.optimization_barrier((term, home))
    by_zhi = [
        [(x * ZHI + z) * CORES + k for z in range(ZHI)] for x in range(X) for k in range(CORES)
    ]
    term = lax.all_to_all(term, "scene", 0, 0, tiled=True, axis_index_groups=by_zhi)
    term = jnp.sum(term.astype(F32), axis=0).astype(BF)
    term = term.reshape(own, ZLO, COLS).transpose(1, 0, 2)
    by_zlo = [[z * Y + y for z in range(ZLO)] for y in range(Y)]
    term = lax.all_to_all(term, "view", 0, 0, tiled=True, axis_index_groups=by_zlo)
    share = jnp.sum(term.astype(F32), axis=0) * float(scenes * VIEWS * TOK) ** (-0.5)
    gq, gk, gv = call(unpack_kernel, (shape(TOK, INNER),) * 3, (home,))
    return (layer[None, None], gq[None, None], gk[None, None], gv[None, None], share)


def solution(mesh):
    rows = P("scene", "view", None, None)
    return jax.shard_map(
        on_device,
        mesh=mesh,
        in_specs=(rows, rows, rows, rows, P(), P("scene", None, None), rows),
        out_specs=(rows, rows, rows, rows, P("scene", "view")),
        check_vma=False,
    )
```

```python
import jax
import jax.numpy as jnp
from jax import lax
from jax.experimental import pallas as pl
from jax.experimental.pallas import tpu as pltpu
from jax.sharding import PartitionSpec as P

HEADS = 8
HEAD_DIM = 64
BLK = 128
TOK = 256
VIEWS = 16
INNER = 512
D = 1024
KEYS = TOK + VIEWS * BLK
WIDE = 2 * HEAD_DIM
COLS = D // VIEWS
BF = jnp.bfloat16
F32 = jnp.float32
SCALE = HEAD_DIM ** (-0.5)
SIDES = 2
PACK_ROWS = TOK + 16
CHUNK = 768
BACK_CHUNK = 256
BACK_ROWS = TOK + BLK
X, ZHI, CORES = 4, 4, 2
ZLO, Y = 4, 4
NT = (((1,), (1,)), ((), ()))
VMEM = pl.BlockSpec(memory_space=pltpu.VMEM)
SMEM = pl.BlockSpec(memory_space=pltpu.SMEM)


def pack_keys_kernel(k_ref, v_ref, out_ref):
    for h in range(HEADS):
        c = slice(h * HEAD_DIM, (h + 1) * HEAD_DIM)
        kv = jnp.concatenate([k_ref[:, c], v_ref[:, c]], axis=1)
        for u in range(SIDES):
            out_ref[u * HEADS + h, :, :] = kv


def pack_queries_kernel(q_ref, go_ref, w_ref, mask_ref, out_ref):
    ga = lax.dot_general(go_ref[...], w_ref[...], NT, preferred_element_type=F32).astype(BF)
    q = q_ref[...] * jnp.asarray(SCALE, BF)
    reads = jnp.concatenate(
        [jnp.broadcast_to(mask_ref[b : b + 1, :], (8, VIEWS)) for b in range(2)], axis=0
    ).astype(BF)
    for h in range(HEADS):
        c = slice(h * HEAD_DIM, (h + 1) * HEAD_DIM)
        out_ref[h, 0:TOK, :] = jnp.concatenate([q[:, c], ga[:, c]], axis=1)
        out_ref[h, TOK:PACK_ROWS, 0:VIEWS] = reads


def rows_of(v, w, fetch_ref):
    return pl.ds(pl.multiple_of(fetch_ref[v * VIEWS + w] * BLK, BLK), BLK)


def gather_rows(v, in_ref, dst, fetch_ref):
    dst[0:TOK, :] = in_ref[v, :, :]
    for w in range(VIEWS):
        dst[TOK + w * BLK : TOK + (w + 1) * BLK, :] = in_ref[w, rows_of(v, w, fetch_ref), :]


def gather_cols(v, src, dst, dims, fetch_ref):
    dst[dims, 0:TOK] = src[:, pl.ds(pl.multiple_of(v * TOK, TOK), TOK)]
    for w in range(VIEWS):
        at = pl.multiple_of(w * TOK + fetch_ref[v * VIEWS + w] * BLK, BLK)
        dst[dims, TOK + w * BLK : TOK + (w + 1) * BLK] = src[:, pl.ds(at, BLK)]


def masked(s, v, w, source, mask_ref):
    parts = []
    for b in range(2):
        seen = jnp.logical_and(mask_ref[(source * 2 + b) * VIEWS + w] == 1, w != v)
        parts.append(s[:, b * BLK : (b + 1) * BLK] + jnp.where(seen, 0.0, -jnp.inf))
    return jnp.concatenate(parts, axis=1)


def side_by_side(t):
    return jnp.concatenate([t[:, :BLK], t[:, BLK:]], axis=0).T


def halves(qg):
    lane = lax.broadcasted_iota(jnp.int32, (TOK, WIDE), 1)
    zero = jnp.zeros_like(qg)
    return jnp.where(lane < HEAD_DIM, qg, zero), jnp.where(lane >= HEAD_DIM, qg, zero)


def place_queries(place_ref, pieces, qg_ref):
    for d, piece in enumerate(pieces):
        at = lax.rem(place_ref[1] - d + HEADS, HEADS)
        qg_ref[at, :, :] = piece[0:TOK, :]


def forward_kernel(fetch_ref, mask_ref, place_ref, in_ref, *refs):
    attn_ref, stat_ref, qg_ref, vt, vsel, s_ref, e_ref, top_ref, kall = refs[HEADS:]
    place_queries(place_ref, refs[:HEADS], qg_ref)
    for w in range(VIEWS):
        vt[:, w * TOK : (w + 1) * TOK] = in_ref[w, :, :].T[HEAD_DIM:, :]
    vsel[0:HEAD_DIM, :] = jnp.ones((HEAD_DIM, KEYS), BF)

    def scores(i, slot):
        v = place_ref[0] + i
        source = lax.rem(place_ref[1] - i + HEADS, HEADS)
        qs = halves(qg_ref[i])[0]
        gather_rows(v, in_ref, kall.at[slot], fetch_ref)
        top = None
        for c in range(0, KEYS, CHUNK):
            r = lax.dot_general(
                kall[slot, c : c + CHUNK, :], qs, NT, preferred_element_type=F32
            )
            for b in range(0, CHUNK, BLK):
                s = r[b : b + BLK, :]
                w = (c + b - TOK) // BLK
                if w >= 0:
                    s = masked(s, v, w, source, mask_ref)
                s_ref[slot, c + b : c + b + BLK, :] = s
                best = jnp.max(s.reshape(BLK // 8, 8, TOK), axis=0)
                top = best if top is None else jnp.maximum(top, best)
        top_ref[slot, 0:1, :] = jnp.max(top, axis=0, keepdims=True)

    def output(i, slot):
        gather_cols(place_ref[0] + i, vt, vsel, slice(HEAD_DIM, WIDE), fetch_ref)
        top = top_ref[slot, 0:1, :]
        for c in range(KEYS // BLK):
            rows = slice(c * BLK, (c + 1) * BLK)
            e_ref[slot, rows, :] = jnp.exp(s_ref[slot, rows, :] - top).astype(BF)
        o = jnp.dot(vsel[...], e_ref[slot], preferred_element_type=F32)
        share = 1.0 / o[0:1, :]
        attn = o[HEAD_DIM:, :] * share
        attn_ref[i, :, :] = side_by_side(attn).astype(BF)
        delta = jnp.sum(attn * qg_ref[i].T[HEAD_DIM:, :].astype(F32), axis=0, keepdims=True)
        stat_ref[i, 0:1, :] = top
        stat_ref[i, 1:2, :] = share
        stat_ref[i, 2:3, :] = delta

    def two_views(n, carry):
        i = 2 * n
        scores(i + 1, 1)
        output(i, 0)
        scores(jnp.minimum(i + 2, HEADS - 1), 0)
        output(i + 1, 1)
        return carry

    scores(0, 0)
    lax.fori_loop(0, HEADS // 2, two_views, 0)


def backward_kernel(
    fetch_ref, mask_ref, place_ref, in_ref, qg_ref, stat_ref, out_ref, kt, ksel, x_ref, acc, kall, qg2_ref
):
    for w in range(VIEWS):
        kt[:, w * TOK : (w + 1) * TOK] = in_ref[w, :, :].T[:HEAD_DIM, :]
        acc[w] = jnp.zeros((TOK, WIDE), F32)
        out_ref[w, TOK:BACK_ROWS, :] = jnp.zeros((BLK, WIDE), BF)

    def weights(i, slot):
        v = place_ref[0] + i
        source = lax.rem(place_ref[1] - i + HEADS, HEADS)
        low, high = halves(qg_ref[i])
        qg2_ref[slot, 0:TOK, :] = low
        qg2_ref[slot, TOK:, :] = high
        qg2 = qg2_ref[slot]
        top = stat_ref[i, 0:1, :]
        share = stat_ref[i, 1:2, :]
        delta = stat_ref[i, 2:3, :]
        gather_rows(v, in_ref, kall.at[slot], fetch_ref)
        for c in range(0, KEYS, BACK_CHUNK):
            r = lax.dot_general(
                kall[slot, c : c + BACK_CHUNK, :], qg2, NT, preferred_element_type=F32
            )
            for b in range(0, BACK_CHUNK, BLK):
                rows = slice(c + b, c + b + BLK)
                s = r[b : b + BLK, 0:TOK]
                w = (c + b - TOK) // BLK
                if w >= 0:
                    s = masked(s, v, w, source, mask_ref)
                prob = jnp.exp(s - top) * share
                x_ref[slot, rows, 0:TOK] = (prob * (r[b : b + BLK, TOK:] - delta)).astype(BF)
                x_ref[slot, rows, TOK:] = prob.astype(BF)

    def sums(i, slot):
        v = place_ref[0] + i
        for c in range(0, KEYS, BACK_CHUNK):
            g = jnp.dot(
                x_ref[slot, c : c + BACK_CHUNK, :], qg2_ref[slot], preferred_element_type=F32
            )
            for b in range(0, BACK_CHUNK, BLK):
                w = (c + b - TOK) // BLK
                if w >= 0:
                    acc[w, rows_of(v, w, fetch_ref), :] += g[b : b + BLK, :]
                else:
                    acc[v, c + b : c + b + BLK, :] += g[b : b + BLK, :]
        gather_cols(v, kt, ksel, slice(0, HEAD_DIM), fetch_ref)
        o = jnp.dot(ksel[...], x_ref[slot, :, 0:TOK], preferred_element_type=F32) * SCALE
        out_ref[v, TOK:BACK_ROWS, :] = side_by_side(o).astype(BF)

    def two_views(n, carry):
        i = 2 * n
        weights(i + 1, 1)
        sums(i, 0)
        weights(jnp.minimum(i + 2, HEADS - 1), 0)
        sums(i + 1, 1)
        return carry

    weights(0, 0)
    lax.fori_loop(0, HEADS // 2, two_views, 0)
    for w in range(VIEWS):
        out_ref[w, 0:TOK, :] = acc[w].astype(BF)


def project_kernel(core_ref, in_ref, go_ref, w_ref, layer_ref, mine_ref, other_ref, attn, term):
    for h in range(HEADS):
        c = slice(h * HEAD_DIM, (h + 1) * HEAD_DIM)
        both = in_ref[h]
        attn[0:BLK, c] = both[:, :HEAD_DIM]
        attn[BLK:, c] = both[:, HEAD_DIM:]
    layer_ref[...] = jnp.dot(attn[...], w_ref[...], preferred_element_type=F32).astype(BF)
    cols = [(z * Y + y) * COLS for y in range(Y) for z in range(ZLO)]
    go = jnp.concatenate([go_ref[:, c : c + COLS] for c in cols], axis=1)
    term[...] = lax.dot_general(
        attn[...], go, (((0,), (0,)), ((), ())), preferred_element_type=F32
    ).astype(BF)
    core = core_ref[0]
    own = INNER // (X * ZHI * CORES)
    wide = ZLO * COLS
    for x in range(X):
        for side, ref in ((core, mine_ref), (1 - core, other_ref)):
            for z in range(ZHI):
                at = pl.multiple_of((x * ZHI + z) * CORES * own + side * own, own)
                rows = term[pl.ds(at, own), :]
                for y in range(Y):
                    ref[x, y, z, :, :] = rows[:, y * wide : (y + 1) * wide]


def unpack_kernel(place_ref, in_ref, gq_ref, gk_ref, gv_ref):
    for h in range(HEADS):
        c = slice(h * HEAD_DIM, (h + 1) * HEAD_DIM)
        kv = in_ref[h, 0:TOK, :].astype(F32) + in_ref[HEADS + h, 0:TOK, :].astype(F32)
        kv = kv.astype(BF)
        gk_ref[:, c] = kv[:, :HEAD_DIM]
        gv_ref[:, c] = kv[:, HEAD_DIM:]
        both = in_ref[place_ref[0] + h, TOK:BACK_ROWS, :]
        gq_ref[0:BLK, c] = both[:, :HEAD_DIM]
        gq_ref[BLK:, c] = both[:, HEAD_DIM:]


def shape(*dims, dtype=BF):
    return jax.ShapeDtypeStruct(dims, dtype)


def call(kernel, outs, args, smem=0, scratch=(), mib=28, flops=0):
    return pl.pallas_call(
        kernel,
        out_shape=outs,
        in_specs=[SMEM] * smem + [VMEM] * (len(args) - smem),
        out_specs=jax.tree.map(lambda _: VMEM, outs),
        scratch_shapes=[pltpu.VMEM(dims, dtype) for dims, dtype in scratch],
        compiler_params=pltpu.CompilerParams(vmem_limit_bytes=mib * 1024 * 1024),
        cost_estimate=pl.CostEstimate(flops=flops, bytes_accessed=4 << 20, transcendentals=0),
    )(*args)


def forward(fetch, reads, place, keys, pieces):
    return call(
        forward_kernel,
        (
            shape(HEADS, BLK, WIDE),
            shape(HEADS, 8, TOK, dtype=F32),
            shape(HEADS, TOK, WIDE),
        ),
        (fetch, reads, place, keys, *pieces),
        smem=3,
        scratch=[
            ((HEAD_DIM, VIEWS * TOK), BF),
            ((WIDE, KEYS), BF),
            ((2, KEYS, TOK), F32),
            ((2, KEYS, TOK), BF),
            ((2, 8, TOK), F32),
            ((2, KEYS, WIDE), BF),
        ],
        flops=10**10,
    )


def backward(fetch, reads, place, keys, queries, stat):
    return call(
        backward_kernel,
        shape(VIEWS, BACK_ROWS, WIDE),
        (fetch, reads, place, keys, queries, stat),
        smem=3,
        scratch=[
            ((HEAD_DIM, VIEWS * TOK), BF),
            ((HEAD_DIM, KEYS), BF),
            ((2, KEYS, 2 * TOK), BF),
            ((VIEWS, TOK, WIDE), F32),
            ((2, KEYS, WIDE), BF),
            ((2, 2 * TOK, WIDE), BF),
        ],
        flops=2 * 10**10,
    )


def swap(rows, axis):
    return lax.all_to_all(rows, axis, split_axis=0, concat_axis=0, tiled=True)


def ring_sum(pieces, axis, count, size, step):
    here = (lax.axis_index(axis) // step) % size
    total = lax.dynamic_index_in_dim(pieces, here, 0, keepdims=False).astype(F32)
    for d in range(1, size):
        pairs = []
        for i in range(count):
            at = (i // step) % size
            pairs.append((i, i + ((at + d) % size - at) * step))
        send = lax.dynamic_index_in_dim(pieces, (here + d) % size, 0, keepdims=False)
        total = total + lax.ppermute(send, axis, pairs).astype(F32)
    return total


def on_device(query_rows, key_rows, value_rows, grad_out, out_weight, fetch_list, read_mask):
    go = grad_out[0, 0]
    fetch = fetch_list.reshape(VIEWS * VIEWS)
    view = lax.axis_index("view")
    side, own_slot = view // HEADS, view % HEADS
    place = jnp.stack([side * HEADS, own_slot]).astype(jnp.int32)
    keys = call(
        pack_keys_kernel, shape(VIEWS, TOK, WIDE), (key_rows[0, 0], value_rows[0, 0]), mib=60
    )
    keys = swap(keys, "view")
    queries = call(
        pack_queries_kernel,
        shape(HEADS, PACK_ROWS, WIDE),
        (query_rows[0, 0], go, out_weight, read_mask[0, 0]),
    )
    pieces = [lax.dynamic_index_in_dim(queries, own_slot, 0, keepdims=False)]
    for d in range(1, HEADS):
        send = lax.dynamic_index_in_dim(queries, (own_slot + d) % HEADS, 0, keepdims=False)
        pairs = [(a, a // HEADS * HEADS + (a % HEADS + d) % HEADS) for a in range(VIEWS)]
        pieces.append(lax.ppermute(send, "view", pairs))
    reads = [piece[r : r + 1, :VIEWS] for piece in pieces for r in (TOK, TOK + 8)]
    reads = jnp.concatenate(reads, axis=0).astype(jnp.int32).reshape(HEADS * 2 * VIEWS)
    attn, stat, queries = forward(fetch, reads, place, keys, pieces)
    sides = [list(range(u * HEADS, (u + 1) * HEADS)) for u in range(SIDES)]
    attn_home = lax.all_to_all(attn, "view", 0, 0, tiled=True, axis_index_groups=sides)
    back = backward(fetch, reads, place, keys, queries, stat)
    attn_home, back = lax.optimization_barrier((attn_home, back))
    core = (lax.axis_index("scene") % CORES).astype(jnp.int32)[None]
    own = INNER // (X * ZHI * CORES)
    piece = shape(X, Y, ZHI, own, ZLO * COLS)
    layer, mine, other = call(
        project_kernel,
        (shape(TOK, D), piece, piece),
        (core, attn_home, go, out_weight),
        smem=1,
        scratch=[((TOK, INNER), BF), ((INNER, D), BF)],
        flops=10**9,
    )
    home = swap(back, "view")
    scenes = X * ZHI * CORES
    other = lax.ppermute(other, "scene", [(i, i ^ 1) for i in range(scenes)])
    term = (mine.astype(F32) + other.astype(F32)).astype(BF)
    term = ring_sum(term, "scene", scenes, X, ZHI * CORES).astype(BF)
    term = ring_sum(term, "view", VIEWS, Y, 1).astype(BF)
    term, home = lax.optimization_barrier((term, home))
    term = term.reshape(ZHI, own, ZLO, COLS).transpose(0, 2, 1, 3).reshape(ZHI * ZLO, own, COLS)
    along_z = [
        [((x * ZHI + zh) * CORES + k) * VIEWS + zl * Y + y for zh in range(ZHI) for zl in range(ZLO)]
        for x in range(X)
        for k in range(CORES)
        for y in range(Y)
    ]
    term = lax.all_to_all(
        term, ("scene", "view"), 0, 0, tiled=True, axis_index_groups=along_z
    )
    share = jnp.sum(term.astype(F32), axis=0) * float(scenes * VIEWS * TOK) ** (-0.5)
    gq, gk, gv = call(unpack_kernel, (shape(TOK, INNER),) * 3, (place, home), smem=1)
    return (layer[None, None], gq[None, None], gk[None, None], gv[None, None], share)


def solution(mesh):
    rows = P("scene", "view", None, None)
    return jax.shard_map(
        on_device,
        mesh=mesh,
        in_specs=(rows, rows, rows, rows, P(), P("scene", None, None), rows),
        out_specs=(rows, rows, rows, rows, P("scene", "view")),
        check_vma=False,
    )
```

```python
import jax
import jax.numpy as jnp
from jax import lax
from jax.experimental import pallas as pl
from jax.experimental.pallas import tpu as pltpu
from jax.sharding import PartitionSpec as P

HEADS = 8
HEAD_DIM = 64
BLK = 128
TOK = 256
VIEWS = 16
INNER = 512
D = 1024
KEYS = TOK + VIEWS * BLK
WIDE = 2 * HEAD_DIM
COLS = D // VIEWS
BF = jnp.bfloat16
F32 = jnp.float32
SCALE = HEAD_DIM ** (-0.5)
SIDES = 2
PACK_ROWS = TOK + 16
CHUNK = 384
BACK_CHUNK = 256
BACK_ROWS = TOK + BLK
X, ZHI, CORES = 4, 4, 2
ZLO, Y = 4, 4
NT = (((1,), (1,)), ((), ()))
VMEM = pl.BlockSpec(memory_space=pltpu.VMEM)
SMEM = pl.BlockSpec(memory_space=pltpu.SMEM)


def pack_keys_kernel(k_ref, v_ref, out_ref):
    for h in range(HEADS):
        c = slice(h * HEAD_DIM, (h + 1) * HEAD_DIM)
        kv = jnp.concatenate([k_ref[:, c], v_ref[:, c]], axis=1)
        for u in range(SIDES):
            out_ref[u * HEADS + h, :, :] = kv


def pack_queries_kernel(q_ref, go_ref, w_ref, mask_ref, out_ref):
    ga = lax.dot_general(go_ref[...], w_ref[...], NT, preferred_element_type=F32).astype(BF)
    q = q_ref[...] * jnp.asarray(SCALE, BF)
    reads = jnp.concatenate(
        [jnp.broadcast_to(mask_ref[b : b + 1, :], (8, VIEWS)) for b in range(2)], axis=0
    ).astype(BF)
    for h in range(HEADS):
        c = slice(h * HEAD_DIM, (h + 1) * HEAD_DIM)
        out_ref[h, 0:TOK, :] = jnp.concatenate([q[:, c], ga[:, c]], axis=1)
        out_ref[h, TOK:PACK_ROWS, 0:VIEWS] = reads


def rows_of(v, w, fetch_ref):
    return pl.ds(pl.multiple_of(fetch_ref[v * VIEWS + w] * BLK, BLK), BLK)


def gather_rows(v, in_ref, dst, fetch_ref):
    dst[0:TOK, :] = in_ref[v, :, :]
    for w in range(VIEWS):
        dst[TOK + w * BLK : TOK + (w + 1) * BLK, :] = in_ref[w, rows_of(v, w, fetch_ref), :]


def gather_cols(v, src, dst, dims, fetch_ref):
    dst[dims, 0:TOK] = src[:, pl.ds(pl.multiple_of(v * TOK, TOK), TOK)]
    for w in range(VIEWS):
        at = pl.multiple_of(w * TOK + fetch_ref[v * VIEWS + w] * BLK, BLK)
        dst[dims, TOK + w * BLK : TOK + (w + 1) * BLK] = src[:, pl.ds(at, BLK)]


def masked(s, v, w, source, mask_ref):
    parts = []
    for b in range(2):
        seen = jnp.logical_and(mask_ref[(source * 2 + b) * VIEWS + w] == 1, w != v)
        parts.append(s[:, b * BLK : (b + 1) * BLK] + jnp.where(seen, 0.0, -jnp.inf))
    return jnp.concatenate(parts, axis=1)


def side_by_side(t):
    return jnp.concatenate([t[:, :BLK], t[:, BLK:]], axis=0).T


def halves(qg):
    lane = lax.broadcasted_iota(jnp.int32, (TOK, WIDE), 1)
    zero = jnp.zeros_like(qg)
    return jnp.where(lane < HEAD_DIM, qg, zero), jnp.where(lane >= HEAD_DIM, qg, zero)


def place_queries(place_ref, near, far_ref, qg_ref):
    for d, piece in enumerate(near):
        along = lax.rem(place_ref[2] - d + Y, Y)
        qg_ref[place_ref[1] * Y + along, :, :] = piece[0:TOK, :]
        qg_ref[(1 - place_ref[1]) * Y + along, :, :] = far_ref[d, 0:TOK, :]


def source_of(i, place_ref):
    row, along = lax.div(i, Y), lax.rem(i, Y)
    return jnp.where(row == place_ref[1], 0, Y) + lax.rem(place_ref[2] - along + Y, Y)


def forward_kernel(fetch_ref, mask_ref, place_ref, in_ref, *refs):
    attn_ref, stat_ref, qg_ref, vt, vsel, s_ref, e_ref, top_ref, kall = refs[Y + 1 :]
    place_queries(place_ref, refs[:Y], refs[Y], qg_ref)
    for w in range(VIEWS):
        vt[:, w * TOK : (w + 1) * TOK] = in_ref[w, :, :].T[HEAD_DIM:, :]
    vsel[0:HEAD_DIM, :] = jnp.ones((HEAD_DIM, KEYS), BF)

    def scores(i, slot):
        v = place_ref[0] + i
        source = source_of(i, place_ref)
        qs = halves(qg_ref[i])[0]
        gather_rows(v, in_ref, kall.at[slot], fetch_ref)
        top = None
        for c in range(0, KEYS, CHUNK):
            r = lax.dot_general(
                kall[slot, c : c + CHUNK, :], qs, NT, preferred_element_type=F32
            )
            for b in range(0, CHUNK, BLK):
                s = r[b : b + BLK, :]
                w = (c + b - TOK) // BLK
                if w >= 0:
                    s = masked(s, v, w, source, mask_ref)
                s_ref[slot, c + b : c + b + BLK, :] = s
                best = jnp.max(s.reshape(BLK // 8, 8, TOK), axis=0)
                top = best if top is None else jnp.maximum(top, best)
        top_ref[slot, 0:1, :] = jnp.max(top, axis=0, keepdims=True)

    def output(i, slot):
        gather_cols(place_ref[0] + i, vt, vsel, slice(HEAD_DIM, WIDE), fetch_ref)
        top = top_ref[slot, 0:1, :]
        for c in range(KEYS // BLK):
            rows = slice(c * BLK, (c + 1) * BLK)
            e_ref[slot, rows, :] = jnp.exp(s_ref[slot, rows, :] - top).astype(BF)
        o = jnp.dot(vsel[...], e_ref[slot], preferred_element_type=F32)
        share = 1.0 / o[0:1, :]
        attn = o[HEAD_DIM:, :] * share
        attn_ref[i, :, :] = side_by_side(attn).astype(BF)
        delta = jnp.sum(attn * qg_ref[i].T[HEAD_DIM:, :].astype(F32), axis=0, keepdims=True)
        stat_ref[i, 0:1, :] = top
        stat_ref[i, 1:2, :] = share
        stat_ref[i, 2:3, :] = delta

    def two_views(n, carry):
        i = 2 * n
        scores(i + 1, 1)
        output(i, 0)
        scores(jnp.minimum(i + 2, HEADS - 1), 0)
        output(i + 1, 1)
        return carry

    scores(0, 0)
    lax.fori_loop(0, HEADS // 2, two_views, 0)


def backward_kernel(
    fetch_ref, mask_ref, place_ref, in_ref, qg_ref, stat_ref, out_ref, kt, ksel, x_ref, acc, kall, qg2_ref
):
    for w in range(VIEWS):
        kt[:, w * TOK : (w + 1) * TOK] = in_ref[w, :, :].T[:HEAD_DIM, :]
        acc[w] = jnp.zeros((TOK, WIDE), F32)
        out_ref[w, TOK:BACK_ROWS, :] = jnp.zeros((BLK, WIDE), BF)

    def weights(i, slot):
        v = place_ref[0] + i
        source = source_of(i, place_ref)
        low, high = halves(qg_ref[i])
        qg2_ref[slot, 0:TOK, :] = low
        qg2_ref[slot, TOK:, :] = high
        qg2 = qg2_ref[slot]
        top = stat_ref[i, 0:1, :]
        share = stat_ref[i, 1:2, :]
        delta = stat_ref[i, 2:3, :]
        gather_rows(v, in_ref, kall.at[slot], fetch_ref)
        for c in range(0, KEYS, BACK_CHUNK):
            r = lax.dot_general(
                kall[slot, c : c + BACK_CHUNK, :], qg2, NT, preferred_element_type=F32
            )
            for b in range(0, BACK_CHUNK, BLK):
                rows = slice(c + b, c + b + BLK)
                s = r[b : b + BLK, 0:TOK]
                w = (c + b - TOK) // BLK
                if w >= 0:
                    s = masked(s, v, w, source, mask_ref)
                prob = jnp.exp(s - top) * share
                x_ref[slot, rows, 0:TOK] = (prob * (r[b : b + BLK, TOK:] - delta)).astype(BF)
                x_ref[slot, rows, TOK:] = prob.astype(BF)

    def sums(i, slot):
        v = place_ref[0] + i
        for c in range(0, KEYS, BACK_CHUNK):
            g = jnp.dot(
                x_ref[slot, c : c + BACK_CHUNK, :], qg2_ref[slot], preferred_element_type=F32
            )
            for b in range(0, BACK_CHUNK, BLK):
                w = (c + b - TOK) // BLK
                if w >= 0:
                    acc[w, rows_of(v, w, fetch_ref), :] += g[b : b + BLK, :]
                else:
                    acc[v, c + b : c + b + BLK, :] += g[b : b + BLK, :]
        gather_cols(v, kt, ksel, slice(0, HEAD_DIM), fetch_ref)
        o = jnp.dot(ksel[...], x_ref[slot, :, 0:TOK], preferred_element_type=F32) * SCALE
        out_ref[v, TOK:BACK_ROWS, :] = side_by_side(o).astype(BF)

    def two_views(n, carry):
        i = 2 * n
        weights(i + 1, 1)
        sums(i, 0)
        weights(jnp.minimum(i + 2, HEADS - 1), 0)
        sums(i + 1, 1)
        return carry

    weights(0, 0)
    lax.fori_loop(0, HEADS // 2, two_views, 0)
    for w in range(VIEWS):
        out_ref[w, 0:TOK, :] = acc[w].astype(BF)


def project_kernel(core_ref, in_ref, go_ref, w_ref, layer_ref, mine_ref, other_ref, attn, term):
    for h in range(HEADS):
        c = slice(h * HEAD_DIM, (h + 1) * HEAD_DIM)
        both = in_ref[h]
        attn[0:BLK, c] = both[:, :HEAD_DIM]
        attn[BLK:, c] = both[:, HEAD_DIM:]
    layer_ref[...] = jnp.dot(attn[...], w_ref[...], preferred_element_type=F32).astype(BF)
    cols = [(z * Y + y) * COLS for y in range(Y) for z in range(ZLO)]
    go = jnp.concatenate([go_ref[:, c : c + COLS] for c in cols], axis=1)
    term[...] = lax.dot_general(
        attn[...], go, (((0,), (0,)), ((), ())), preferred_element_type=F32
    ).astype(BF)
    core = core_ref[0]
    own = INNER // (X * ZHI * CORES)
    wide = ZLO * COLS
    for x in range(X):
        for side, ref in ((core, mine_ref), (1 - core, other_ref)):
            for z in range(ZHI):
                at = pl.multiple_of((x * ZHI + z) * CORES * own + side * own, own)
                rows = term[pl.ds(at, own), :]
                for y in range(Y):
                    ref[x, y, z, :, :] = rows[:, y * wide : (y + 1) * wide]


def unpack_kernel(place_ref, in_ref, gq_ref, gk_ref, gv_ref):
    for h in range(HEADS):
        c = slice(h * HEAD_DIM, (h + 1) * HEAD_DIM)
        kv = in_ref[h, 0:TOK, :].astype(F32) + in_ref[HEADS + h, 0:TOK, :].astype(F32)
        kv = kv.astype(BF)
        gk_ref[:, c] = kv[:, :HEAD_DIM]
        gv_ref[:, c] = kv[:, HEAD_DIM:]
        both = in_ref[place_ref[0] + h, TOK:BACK_ROWS, :]
        gq_ref[0:BLK, c] = both[:, :HEAD_DIM]
        gq_ref[BLK:, c] = both[:, HEAD_DIM:]


def shape(*dims, dtype=BF):
    return jax.ShapeDtypeStruct(dims, dtype)


def call(kernel, outs, args, smem=0, scratch=(), mib=28, flops=0):
    return pl.pallas_call(
        kernel,
        out_shape=outs,
        in_specs=[SMEM] * smem + [VMEM] * (len(args) - smem),
        out_specs=jax.tree.map(lambda _: VMEM, outs),
        scratch_shapes=[pltpu.VMEM(dims, dtype) for dims, dtype in scratch],
        compiler_params=pltpu.CompilerParams(vmem_limit_bytes=mib * 1024 * 1024),
        cost_estimate=pl.CostEstimate(flops=flops, bytes_accessed=4 << 20, transcendentals=0),
    )(*args)


def forward(fetch, reads, place, keys, pieces):
    return call(
        forward_kernel,
        (
            shape(HEADS, BLK, WIDE),
            shape(HEADS, 8, TOK, dtype=F32),
            shape(HEADS, TOK, WIDE),
        ),
        (fetch, reads, place, keys, *pieces),
        smem=3,
        scratch=[
            ((HEAD_DIM, VIEWS * TOK), BF),
            ((WIDE, KEYS), BF),
            ((2, KEYS, TOK), F32),
            ((2, KEYS, TOK), BF),
            ((2, 8, TOK), F32),
            ((2, KEYS, WIDE), BF),
        ],
        flops=10**10,
    )


def backward(fetch, reads, place, keys, queries, stat):
    return call(
        backward_kernel,
        shape(VIEWS, BACK_ROWS, WIDE),
        (fetch, reads, place, keys, queries, stat),
        smem=3,
        scratch=[
            ((HEAD_DIM, VIEWS * TOK), BF),
            ((HEAD_DIM, KEYS), BF),
            ((2, KEYS, 2 * TOK), BF),
            ((VIEWS, TOK, WIDE), F32),
            ((2, KEYS, WIDE), BF),
            ((2, 2 * TOK, WIDE), BF),
        ],
        flops=2 * 10**10,
    )


def swap(rows, axis):
    return lax.all_to_all(rows, axis, split_axis=0, concat_axis=0, tiled=True)


def ring_sum(pieces, axis, count, size, step):
    here = (lax.axis_index(axis) // step) % size
    total = lax.dynamic_index_in_dim(pieces, here, 0, keepdims=False).astype(F32)
    for d in range(1, size):
        pairs = []
        for i in range(count):
            at = (i // step) % size
            pairs.append((i, i + ((at + d) % size - at) * step))
        send = lax.dynamic_index_in_dim(pieces, (here + d) % size, 0, keepdims=False)
        total = total + lax.ppermute(send, axis, pairs).astype(F32)
    return total


def on_device(query_rows, key_rows, value_rows, grad_out, out_weight, fetch_list, read_mask):
    go = grad_out[0, 0]
    fetch = fetch_list.reshape(VIEWS * VIEWS)
    view = lax.axis_index("view")
    side, row, along = view // HEADS, view // Y % 2, view % Y
    place = jnp.stack([side * HEADS, row, along]).astype(jnp.int32)
    keys = call(
        pack_keys_kernel, shape(VIEWS, TOK, WIDE), (key_rows[0, 0], value_rows[0, 0]), mib=60
    )
    keys = swap(keys, "view")
    queries = call(
        pack_queries_kernel,
        shape(HEADS, PACK_ROWS, WIDE),
        (query_rows[0, 0], go, out_weight, read_mask[0, 0]),
    )
    queries = queries.reshape(2, Y, PACK_ROWS, WIDE)
    moved = [lax.dynamic_index_in_dim(queries, along, 1, keepdims=False)]
    for d in range(1, Y):
        send = lax.dynamic_index_in_dim(queries, (along + d) % Y, 1, keepdims=False)
        pairs = [(a, a // Y * Y + (a % Y + d) % Y) for a in range(VIEWS)]
        moved.append(lax.ppermute(send, "view", pairs))
    near = [lax.dynamic_index_in_dim(m, row, 0, keepdims=False) for m in moved]
    far = jnp.stack([lax.dynamic_index_in_dim(m, 1 - row, 0, keepdims=False) for m in moved])
    far = lax.ppermute(far, "view", [(a, a ^ Y) for a in range(VIEWS)])
    reads = [piece[None] for piece in near] + [far]
    reads = [piece[:, TOK::8, :VIEWS] for piece in reads]
    reads = jnp.concatenate(reads, axis=0).astype(jnp.int32).reshape(HEADS * 2 * VIEWS)
    pieces = near + [far]
    attn, stat, queries = forward(fetch, reads, place, keys, pieces)
    sides = [list(range(u * HEADS, (u + 1) * HEADS)) for u in range(SIDES)]
    attn_home = lax.all_to_all(attn, "view", 0, 0, tiled=True, axis_index_groups=sides)
    back = backward(fetch, reads, place, keys, queries, stat)
    attn_home, back = lax.optimization_barrier((attn_home, back))
    core = (lax.axis_index("scene") % CORES).astype(jnp.int32)[None]
    own = INNER // (X * ZHI * CORES)
    piece = shape(X, Y, ZHI, own, ZLO * COLS)
    layer, mine, other = call(
        project_kernel,
        (shape(TOK, D), piece, piece),
        (core, attn_home, go, out_weight),
        smem=1,
        scratch=[((TOK, INNER), BF), ((INNER, D), BF)],
        flops=10**9,
    )
    home = swap(back, "view")
    scenes = X * ZHI * CORES
    other = lax.ppermute(other, "scene", [(i, i ^ 1) for i in range(scenes)])
    term = (mine.astype(F32) + other.astype(F32)).astype(BF)
    term = ring_sum(term, "scene", scenes, X, ZHI * CORES).astype(BF)
    term = ring_sum(term, "view", VIEWS, Y, 1).astype(BF)
    term, home = lax.optimization_barrier((term, home))
    term = term.reshape(ZHI, own, ZLO, COLS).transpose(0, 2, 1, 3).reshape(ZHI * ZLO, own, COLS)
    along_z = [
        [((x * ZHI + zh) * CORES + k) * VIEWS + zl * Y + y for zh in range(ZHI) for zl in range(ZLO)]
        for x in range(X)
        for k in range(CORES)
        for y in range(Y)
    ]
    term = lax.all_to_all(
        term, ("scene", "view"), 0, 0, tiled=True, axis_index_groups=along_z
    )
    share = jnp.sum(term.astype(F32), axis=0) * float(scenes * VIEWS * TOK) ** (-0.5)
    gq, gk, gv = call(unpack_kernel, (shape(TOK, INNER),) * 3, (place, home), smem=1)
    return (layer[None, None], gq[None, None], gk[None, None], gv[None, None], share)


def solution(mesh):
    rows = P("scene", "view", None, None)
    return jax.shard_map(
        on_device,
        mesh=mesh,
        in_specs=(rows, rows, rows, rows, P(), P("scene", None, None), rows),
        out_specs=(rows, rows, rows, rows, P("scene", "view")),
        check_vma=False,
    )
```

```python
import jax
import jax.numpy as jnp
from jax import lax
from jax.experimental import pallas as pl
from jax.experimental.pallas import tpu as pltpu
from jax.sharding import PartitionSpec as P

HEADS = 8
HEAD_DIM = 64
BLK = 128
TOK = 256
VIEWS = 16
INNER = 512
D = 1024
KEYS = TOK + VIEWS * BLK
WIDE = 2 * HEAD_DIM
COLS = D // VIEWS
BF = jnp.bfloat16
F32 = jnp.float32
SCALE = HEAD_DIM ** (-0.5)
SIDES = 2
PACK_ROWS = TOK + 16
CHUNK = 384
BACK_CHUNK = 256
BACK_ROWS = TOK + BLK
X, ZHI, CORES = 4, 4, 2
ZLO, Y = 4, 4
NT = (((1,), (1,)), ((), ()))
VMEM = pl.BlockSpec(memory_space=pltpu.VMEM)
SMEM = pl.BlockSpec(memory_space=pltpu.SMEM)


def pack_keys_kernel(k_ref, v_ref, out_ref):
    for h in range(HEADS):
        c = slice(h * HEAD_DIM, (h + 1) * HEAD_DIM)
        kv = jnp.concatenate([k_ref[:, c], v_ref[:, c]], axis=1)
        for u in range(SIDES):
            out_ref[u * HEADS + h, :, :] = kv


def pack_queries_kernel(q_ref, go_ref, w_ref, mask_ref, out_ref):
    ga = lax.dot_general(go_ref[...], w_ref[...], NT, preferred_element_type=F32).astype(BF)
    q = q_ref[...] * jnp.asarray(SCALE, BF)
    reads = jnp.concatenate(
        [jnp.broadcast_to(mask_ref[b : b + 1, :], (8, VIEWS)) for b in range(2)], axis=0
    ).astype(BF)
    for h in range(HEADS):
        c = slice(h * HEAD_DIM, (h + 1) * HEAD_DIM)
        out_ref[h, 0:TOK, :] = jnp.concatenate([q[:, c], ga[:, c]], axis=1)
        out_ref[h, TOK:PACK_ROWS, 0:VIEWS] = reads


def rows_of(v, w, fetch_ref):
    return pl.ds(pl.multiple_of(fetch_ref[v * VIEWS + w] * BLK, BLK), BLK)


def gather_rows(v, in_ref, dst, fetch_ref):
    dst[0:TOK, :] = in_ref[v, :, :]
    for w in range(VIEWS):
        dst[TOK + w * BLK : TOK + (w + 1) * BLK, :] = in_ref[w, rows_of(v, w, fetch_ref), :]


def gather_cols(v, src, dst, dims, fetch_ref):
    dst[dims, 0:TOK] = src[:, pl.ds(pl.multiple_of(v * TOK, TOK), TOK)]
    for w in range(VIEWS):
        at = pl.multiple_of(w * TOK + fetch_ref[v * VIEWS + w] * BLK, BLK)
        dst[dims, TOK + w * BLK : TOK + (w + 1) * BLK] = src[:, pl.ds(at, BLK)]


def masked(s, v, w, source, mask_ref):
    parts = []
    for b in range(2):
        seen = jnp.logical_and(mask_ref[(source * 2 + b) * VIEWS + w] == 1, w != v)
        parts.append(s[:, b * BLK : (b + 1) * BLK] + jnp.where(seen, 0.0, -jnp.inf))
    return jnp.concatenate(parts, axis=1)


def side_by_side(t):
    return jnp.concatenate([t[:, :BLK], t[:, BLK:]], axis=0).T


def halves(qg):
    lane = lax.broadcasted_iota(jnp.int32, (TOK, WIDE), 1)
    zero = jnp.zeros_like(qg)
    return jnp.where(lane < HEAD_DIM, qg, zero), jnp.where(lane >= HEAD_DIM, qg, zero)


def place_queries(place_ref, near, far_ref, qg_ref):
    for d, piece in enumerate(near):
        along = lax.bitwise_xor(place_ref[2], d)
        qg_ref[place_ref[1] * Y + along, :, :] = piece[0:TOK, :]
        qg_ref[(1 - place_ref[1]) * Y + along, :, :] = far_ref[d, 0:TOK, :]


def source_of(i, place_ref):
    row, along = lax.div(i, Y), lax.rem(i, Y)
    return jnp.where(row == place_ref[1], 0, Y) + lax.bitwise_xor(place_ref[2], along)


def forward_kernel(fetch_ref, mask_ref, place_ref, in_ref, *refs):
    attn_ref, stat_ref, qg_ref, vt, vsel, s_ref, e_ref, top_ref, kall = refs[Y + 1 :]
    place_queries(place_ref, refs[:Y], refs[Y], qg_ref)
    for w in range(VIEWS):
        vt[:, w * TOK : (w + 1) * TOK] = in_ref[w, :, :].T[HEAD_DIM:, :]
    vsel[0:HEAD_DIM, :] = jnp.ones((HEAD_DIM, KEYS), BF)

    def scores(i, slot):
        v = place_ref[0] + i
        source = source_of(i, place_ref)
        qs = halves(qg_ref[i])[0]
        gather_rows(v, in_ref, kall.at[slot], fetch_ref)
        top = None
        for c in range(0, KEYS, CHUNK):
            r = lax.dot_general(
                kall[slot, c : c + CHUNK, :], qs, NT, preferred_element_type=F32
            )
            for b in range(0, CHUNK, BLK):
                s = r[b : b + BLK, :]
                w = (c + b - TOK) // BLK
                if w >= 0:
                    s = masked(s, v, w, source, mask_ref)
                s_ref[slot, c + b : c + b + BLK, :] = s
                best = jnp.max(s.reshape(BLK // 8, 8, TOK), axis=0)
                top = best if top is None else jnp.maximum(top, best)
        top_ref[slot, 0:1, :] = jnp.max(top, axis=0, keepdims=True)

    def output(i, slot):
        gather_cols(place_ref[0] + i, vt, vsel, slice(HEAD_DIM, WIDE), fetch_ref)
        top = top_ref[slot, 0:1, :]
        for c in range(KEYS // BLK):
            rows = slice(c * BLK, (c + 1) * BLK)
            e_ref[slot, rows, :] = jnp.exp(s_ref[slot, rows, :] - top).astype(BF)
        o = jnp.dot(vsel[...], e_ref[slot], preferred_element_type=F32)
        share = 1.0 / o[0:1, :]
        attn = o[HEAD_DIM:, :] * share
        attn_ref[i, :, :] = side_by_side(attn).astype(BF)
        delta = jnp.sum(attn * qg_ref[i].T[HEAD_DIM:, :].astype(F32), axis=0, keepdims=True)
        stat_ref[i, 0:1, :] = top
        stat_ref[i, 1:2, :] = share
        stat_ref[i, 2:3, :] = delta

    def two_views(n, carry):
        i = 2 * n
        scores(i + 1, 1)
        output(i, 0)
        scores(jnp.minimum(i + 2, HEADS - 1), 0)
        output(i + 1, 1)
        return carry

    scores(0, 0)
    lax.fori_loop(0, HEADS // 2, two_views, 0)


def backward_kernel(
    fetch_ref, mask_ref, place_ref, in_ref, qg_ref, stat_ref, out_ref, kt, ksel, x_ref, acc, kall, qg2_ref
):
    for w in range(VIEWS):
        kt[:, w * TOK : (w + 1) * TOK] = in_ref[w, :, :].T[:HEAD_DIM, :]
        acc[w] = jnp.zeros((TOK, WIDE), F32)
        out_ref[w, TOK:BACK_ROWS, :] = jnp.zeros((BLK, WIDE), BF)

    def weights(i, slot):
        v = place_ref[0] + i
        source = source_of(i, place_ref)
        low, high = halves(qg_ref[i])
        qg2_ref[slot, 0:TOK, :] = low
        qg2_ref[slot, TOK:, :] = high
        qg2 = qg2_ref[slot]
        top = stat_ref[i, 0:1, :]
        share = stat_ref[i, 1:2, :]
        delta = stat_ref[i, 2:3, :]
        gather_rows(v, in_ref, kall.at[slot], fetch_ref)
        for c in range(0, KEYS, BACK_CHUNK):
            r = lax.dot_general(
                kall[slot, c : c + BACK_CHUNK, :], qg2, NT, preferred_element_type=F32
            )
            for b in range(0, BACK_CHUNK, BLK):
                rows = slice(c + b, c + b + BLK)
                s = r[b : b + BLK, 0:TOK]
                w = (c + b - TOK) // BLK
                if w >= 0:
                    s = masked(s, v, w, source, mask_ref)
                prob = jnp.exp(s - top) * share
                x_ref[slot, rows, 0:TOK] = (prob * (r[b : b + BLK, TOK:] - delta)).astype(BF)
                x_ref[slot, rows, TOK:] = prob.astype(BF)

    def sums(i, slot):
        v = place_ref[0] + i
        for c in range(0, KEYS, BACK_CHUNK):
            g = jnp.dot(
                x_ref[slot, c : c + BACK_CHUNK, :], qg2_ref[slot], preferred_element_type=F32
            )
            for b in range(0, BACK_CHUNK, BLK):
                w = (c + b - TOK) // BLK
                if w >= 0:
                    acc[w, rows_of(v, w, fetch_ref), :] += g[b : b + BLK, :]
                else:
                    acc[v, c + b : c + b + BLK, :] += g[b : b + BLK, :]
        gather_cols(v, kt, ksel, slice(0, HEAD_DIM), fetch_ref)
        o = jnp.dot(ksel[...], x_ref[slot, :, 0:TOK], preferred_element_type=F32) * SCALE
        out_ref[v, TOK:BACK_ROWS, :] = side_by_side(o).astype(BF)

    def two_views(n, carry):
        i = 2 * n
        weights(i + 1, 1)
        sums(i, 0)
        weights(jnp.minimum(i + 2, HEADS - 1), 0)
        sums(i + 1, 1)
        return carry

    weights(0, 0)
    lax.fori_loop(0, HEADS // 2, two_views, 0)
    for w in range(VIEWS):
        out_ref[w, 0:TOK, :] = acc[w].astype(BF)


def project_kernel(core_ref, in_ref, go_ref, w_ref, layer_ref, mine_ref, other_ref, attn, term):
    for h in range(HEADS):
        c = slice(h * HEAD_DIM, (h + 1) * HEAD_DIM)
        both = in_ref[h]
        attn[0:BLK, c] = both[:, :HEAD_DIM]
        attn[BLK:, c] = both[:, HEAD_DIM:]
    layer_ref[...] = jnp.dot(attn[...], w_ref[...], preferred_element_type=F32).astype(BF)
    cols = [(z * Y + y) * COLS for y in range(Y) for z in range(ZLO)]
    go = jnp.concatenate([go_ref[:, c : c + COLS] for c in cols], axis=1)
    term[...] = lax.dot_general(
        attn[...], go, (((0,), (0,)), ((), ())), preferred_element_type=F32
    ).astype(BF)
    core = core_ref[0]
    own = INNER // (X * ZHI * CORES)
    wide = ZLO * COLS
    for x in range(X):
        for side, ref in ((core, mine_ref), (1 - core, other_ref)):
            for z in range(ZHI):
                at = pl.multiple_of((x * ZHI + z) * CORES * own + side * own, own)
                rows = term[pl.ds(at, own), :]
                for y in range(Y):
                    ref[x, y, z, :, :] = rows[:, y * wide : (y + 1) * wide]


def unpack_kernel(place_ref, in_ref, gq_ref, gk_ref, gv_ref):
    for h in range(HEADS):
        c = slice(h * HEAD_DIM, (h + 1) * HEAD_DIM)
        kv = in_ref[h, 0:TOK, :].astype(F32) + in_ref[HEADS + h, 0:TOK, :].astype(F32)
        kv = kv.astype(BF)
        gk_ref[:, c] = kv[:, :HEAD_DIM]
        gv_ref[:, c] = kv[:, HEAD_DIM:]
        both = in_ref[place_ref[0] + h, TOK:BACK_ROWS, :]
        gq_ref[0:BLK, c] = both[:, :HEAD_DIM]
        gq_ref[BLK:, c] = both[:, HEAD_DIM:]


def shape(*dims, dtype=BF):
    return jax.ShapeDtypeStruct(dims, dtype)


def call(kernel, outs, args, smem=0, scratch=(), mib=28, flops=0):
    return pl.pallas_call(
        kernel,
        out_shape=outs,
        in_specs=[SMEM] * smem + [VMEM] * (len(args) - smem),
        out_specs=jax.tree.map(lambda _: VMEM, outs),
        scratch_shapes=[pltpu.VMEM(dims, dtype) for dims, dtype in scratch],
        compiler_params=pltpu.CompilerParams(vmem_limit_bytes=mib * 1024 * 1024),
        cost_estimate=pl.CostEstimate(flops=flops, bytes_accessed=4 << 20, transcendentals=0),
    )(*args)


def forward(fetch, reads, place, keys, pieces):
    return call(
        forward_kernel,
        (
            shape(HEADS, BLK, WIDE),
            shape(HEADS, 8, TOK, dtype=F32),
            shape(HEADS, TOK, WIDE),
        ),
        (fetch, reads, place, keys, *pieces),
        smem=3,
        scratch=[
            ((HEAD_DIM, VIEWS * TOK), BF),
            ((WIDE, KEYS), BF),
            ((2, KEYS, TOK), F32),
            ((2, KEYS, TOK), BF),
            ((2, 8, TOK), F32),
            ((2, KEYS, WIDE), BF),
        ],
        flops=10**10,
    )


def backward(fetch, reads, place, keys, queries, stat):
    return call(
        backward_kernel,
        shape(VIEWS, BACK_ROWS, WIDE),
        (fetch, reads, place, keys, queries, stat),
        smem=3,
        scratch=[
            ((HEAD_DIM, VIEWS * TOK), BF),
            ((HEAD_DIM, KEYS), BF),
            ((2, KEYS, 2 * TOK), BF),
            ((VIEWS, TOK, WIDE), F32),
            ((2, KEYS, WIDE), BF),
            ((2, 2 * TOK, WIDE), BF),
        ],
        flops=2 * 10**10,
    )


def swap(rows, axis):
    return lax.all_to_all(rows, axis, split_axis=0, concat_axis=0, tiled=True)


def ring_sum(pieces, axis, count, size, step):
    here = (lax.axis_index(axis) // step) % size
    total = lax.dynamic_index_in_dim(pieces, here, 0, keepdims=False).astype(F32)
    for d in range(1, size):
        pairs = []
        for i in range(count):
            at = (i // step) % size
            pairs.append((i, i + ((at ^ d) - at) * step))
        send = lax.dynamic_index_in_dim(pieces, here ^ d, 0, keepdims=False)
        total = total + lax.ppermute(send, axis, pairs).astype(F32)
    return total


def on_device(query_rows, key_rows, value_rows, grad_out, out_weight, fetch_list, read_mask):
    go = grad_out[0, 0]
    fetch = fetch_list.reshape(VIEWS * VIEWS)
    view = lax.axis_index("view")
    side, row, along = view // HEADS, view // Y % 2, view % Y
    place = jnp.stack([side * HEADS, row, along]).astype(jnp.int32)
    keys = call(
        pack_keys_kernel, shape(VIEWS, TOK, WIDE), (key_rows[0, 0], value_rows[0, 0]), mib=60
    )
    keys = swap(keys, "view")
    queries = call(
        pack_queries_kernel,
        shape(HEADS, PACK_ROWS, WIDE),
        (query_rows[0, 0], go, out_weight, read_mask[0, 0]),
    )
    queries = queries.reshape(2, Y, PACK_ROWS, WIDE)
    moved = [lax.dynamic_index_in_dim(queries, along, 1, keepdims=False)]
    for d in range(1, Y):
        send = lax.dynamic_index_in_dim(queries, along ^ d, 1, keepdims=False)
        pairs = [(a, a ^ d) for a in range(VIEWS)]
        moved.append(lax.ppermute(send, "view", pairs))
    near = [lax.dynamic_index_in_dim(m, row, 0, keepdims=False) for m in moved]
    far = jnp.stack([lax.dynamic_index_in_dim(m, 1 - row, 0, keepdims=False) for m in moved])
    far = lax.ppermute(far, "view", [(a, a ^ Y) for a in range(VIEWS)])
    reads = [piece[None] for piece in near] + [far]
    reads = [piece[:, TOK::8, :VIEWS] for piece in reads]
    reads = jnp.concatenate(reads, axis=0).astype(jnp.int32).reshape(HEADS * 2 * VIEWS)
    pieces = near + [far]
    attn, stat, queries = forward(fetch, reads, place, keys, pieces)
    sides = [list(range(u * HEADS, (u + 1) * HEADS)) for u in range(SIDES)]
    attn_home = lax.all_to_all(attn, "view", 0, 0, tiled=True, axis_index_groups=sides)
    back = backward(fetch, reads, place, keys, queries, stat)
    attn_home, back = lax.optimization_barrier((attn_home, back))
    core = (lax.axis_index("scene") % CORES).astype(jnp.int32)[None]
    own = INNER // (X * ZHI * CORES)
    piece = shape(X, Y, ZHI, own, ZLO * COLS)
    layer, mine, other = call(
        project_kernel,
        (shape(TOK, D), piece, piece),
        (core, attn_home, go, out_weight),
        smem=1,
        scratch=[((TOK, INNER), BF), ((INNER, D), BF)],
        flops=10**9,
    )
    home = swap(back, "view")
    scenes = X * ZHI * CORES
    other = lax.ppermute(other, "scene", [(i, i ^ 1) for i in range(scenes)])
    term = (mine.astype(F32) + other.astype(F32)).astype(BF)
    term = ring_sum(term, "scene", scenes, X, ZHI * CORES).astype(BF)
    term = ring_sum(term, "view", VIEWS, Y, 1).astype(BF)
    term, home = lax.optimization_barrier((term, home))
    term = term.reshape(ZHI, own, ZLO, COLS).transpose(0, 2, 1, 3).reshape(ZHI * ZLO, own, COLS)
    along_z = [
        [((x * ZHI + zh) * CORES + k) * VIEWS + zl * Y + y for zh in range(ZHI) for zl in range(ZLO)]
        for x in range(X)
        for k in range(CORES)
        for y in range(Y)
    ]
    term = lax.all_to_all(
        term, ("scene", "view"), 0, 0, tiled=True, axis_index_groups=along_z
    )
    share = jnp.sum(term.astype(F32), axis=0) * float(scenes * VIEWS * TOK) ** (-0.5)
    gq, gk, gv = call(unpack_kernel, (shape(TOK, INNER),) * 3, (place, home), smem=1)
    return (layer[None, None], gq[None, None], gk[None, None], gv[None, None], share)


def solution(mesh):
    rows = P("scene", "view", None, None)
    return jax.shard_map(
        on_device,
        mesh=mesh,
        in_specs=(rows, rows, rows, rows, P(), P("scene", None, None), rows),
        out_specs=(rows, rows, rows, rows, P("scene", "view")),
        check_vma=False,
    )
```
